512 devices in a mesh: gx: 4 (over y_lo, core), gy: 4 (over y_hi), gz: 32 (over z, x).
Axes of the slice: x: 4, y: 8 (y_hi: 4, y_lo: 2; y = y_hi * 2 + y_lo), z: 8, core: 2. Of those that a mesh axis runs over, the one named last changes fastest.
Arguments:
- density: float32 [512, 64, 4096], P('gz', 'gx', 'gy'), may hold values from 0.1 to 10
Outputs:
- details_one: float32 [7, 256, 32, 2048], P(None, 'gz', 'gx', 'gy')
- details_two: float32 [7, 128, 16, 1024], P(None, 'gz', 'gx', 'gy')
- details_three: float32 [7, 64, 8, 512], P(None, 'gz', 'gx', 'gy')
- approximation: float32 [64, 8, 512], P('gz', 'gx', 'gy')
The draws below stay inside these ranges and needn't reach their ends.
All inputs are finite; a program needn't handle non-finite values.
Results may differ from the reference program's by a relative error of at most 0.00011.
Values sent between devices are 32-bit elements; how exact they have to be, the bound alone decides.
No kernel may reach another device: no remote copies, remote signals or barrier semaphores. Data moves between devices by JAX's collectives and lax.ppermute only.
A program may use at most 128 MiB of HBM per device.

```python
import math
import jax
import jax.numpy as jnp

NX = 64
NY = 4096
NZ = 512


def shard_levels(own_key, dims, split, smallest, high):
    loudness, own = 1.0, jax.random.fold_in(own_key, 6)
    for axis_at, shards_of in split:
        heights = jnp.exp(jax.random.uniform(jax.random.fold_in(own, axis_at), (shards_of,), jnp.float32, smallest / len(split), high / len(split)))
        loudness = loudness * jnp.repeat(heights, dims[axis_at] // shards_of).reshape([-1 if axis == axis_at else 1 for axis in range(len(dims))])
    return loudness


def setup_inputs(seed: int = 0) -> dict:
    key_of = jax.random.split(jax.random.key(seed), 2)
    density = jnp.clip(jnp.exp(math.log(10.0) - 4.6051702 * jax.random.uniform(key_of[0], (NZ, NX, NY), jnp.float32) ** shard_levels(key_of[0], (NZ, NX, NY), ((0, 32), (1, 4), (2, 4)), -0.2, 0.2)), 0.1, 10.0)
    return dict(density=density)


ALPHA = -1.586134342
BETA = -0.05298011854
GAMMA = 0.8829110762
DELTA = 0.4435068522
ZETA = 1.149604398


def lift_padded(padded, dim):
    moved = jnp.moveaxis(padded, dim, -1)
    half = moved.shape[-1] // 2 - 4
    evens = moved[..., 0::2]
    odds = moved[..., 1::2]
    first_d = odds[..., :half + 3] + ALPHA * (evens[..., :half + 3] + evens[..., 1:half + 4])
    first_s = evens[..., 1:half + 3] + BETA * (first_d[..., :half + 2] + first_d[..., 1:half + 3])
    second_d = first_d[..., 1:half + 2] + GAMMA * (first_s[..., :half + 1] + first_s[..., 1:half + 2])
    second_s = first_s[..., 1:half + 1] + DELTA * (second_d[..., :half] + second_d[..., 1:half + 1])
    lower = jnp.moveaxis(second_s * ZETA, -1, dim)
    upper = jnp.moveaxis(second_d[..., 1:half + 1] / ZETA, -1, dim)
    return jnp.concatenate([lower, upper], axis=0)


def wrap_pad(data, dim):
    widths = [(0, 0)] * data.ndim
    widths[dim] = (4, 4)
    return jnp.pad(data, widths, mode="wrap")


def one_level(data):
    for dim in (2, 3, 1):
        data = lift_padded(wrap_pad(data, dim), dim)
    return data


def reference(density):
    data = density[None]
    results = []
    for level in range(3):
        data = one_level(data)
        results.append(data[1:])
        data = data[0:1]
    return results[0], results[1], results[2], data[0]
```

```python
import functools

import jax
import jax.numpy as jnp
import numpy as np
from jax import lax
from jax.experimental import pallas as pl
from jax.experimental.pallas import tpu as pltpu
from jax.sharding import PartitionSpec as P

ALPHA = -1.586134342
BETA = -0.05298011854
GAMMA = 0.8829110762
DELTA = 0.4435068522
ZETA = 1.149604398

N = 16
F32 = jnp.float32


def plus(a, b):
    if a is None:
        return b
    return a if b is None else a + b


def times(c, a):
    return None if a is None else c * a


class Level:
    def __init__(self, line):
        self.line = line
        self.memo = {}

    def get(self, name, i):
        if (name, i) not in self.memo:
            self.memo[name, i] = getattr(self, name)(i)
        return self.memo[name, i]

    def s0(self, i):
        return self.line(2 * i)

    def d0(self, i):
        return self.line(2 * i + 1)

    def d1(self, i):
        return plus(self.get("d0", i), times(ALPHA, plus(self.get("s0", i), self.get("s0", i + 1))))

    def s1(self, i):
        return plus(self.get("s0", i), times(BETA, plus(self.get("d1", i - 1), self.get("d1", i))))

    def d2(self, i):
        return plus(self.get("d1", i), times(GAMMA, plus(self.get("s1", i), self.get("s1", i + 1))))

    def s2(self, i):
        return plus(self.get("s1", i), times(DELTA, plus(self.get("d2", i - 1), self.get("d2", i))))

    def low(self, i):
        return times(ZETA, self.get("s2", i))

    def high(self, i):
        return times(1.0 / ZETA, self.get("d2", i))


def block_levels(rows, count):
    line = lambda i: rows[i] if 0 <= i < N else None
    for _ in range(count):
        level = Level(line)
        line = functools.partial(level.get, "low")
    return level


BANDS = ("low", "high")


def own_count(count):
    return N >> count


def spill_matrices(count):
    n = own_count(count)
    level = block_levels(list(np.eye(N)), count)
    zero = np.zeros(N)

    def at(band, i):
        value = level.get(band, i)
        return zero if value is None else value

    return {
        offset: np.stack([at(band, offset * n + i) for band in BANDS for i in range(n)])
        for offset in (-2, -1, 1, 2)
    }


def factor(matrix):
    picked, rest = [], matrix.copy()
    scale = np.abs(matrix).max()
    while scale > 0 and np.abs(rest).max() > 1e-10 * scale:
        row = int(np.argmax((rest**2).sum(1)))
        picked.append(row)
        q = rest[row] / np.linalg.norm(rest[row])
        rest = rest - np.outer(rest @ q, q)
    picked.sort()
    if not picked:
        return [], None
    coefs = np.linalg.lstsq(matrix[picked].T, matrix.T, rcond=None)[0].T
    coefs[np.abs(coefs) < 1e-9] = 0.0
    coefs[np.abs(coefs - 1.0) < 1e-9] = 1.0
    return picked, coefs


PLAN = {count: {o: factor(m) for o, m in spill_matrices(count).items()} for count in (1, 2, 3)}
TILES = {1: 8, 2: 4, 3: 2}


def sent(level, count, offset):
    n = own_count(count)
    return [level.get(BANDS[row // n], offset * n + row % n) for row in PLAN[count][offset][0]]


def added(count, offset, row, lines):
    coefs = PLAN[count][offset][1][row]
    total = None
    for c, line in zip(coefs, lines):
        if c != 0.0:
            total = plus(total, line() if c == 1.0 else times(float(c), line()))
    return total


def message_places(height, offsets, counts):
    places, at = {}, 0
    for offset in offsets:
        for count in counts:
            for k in range(len(PLAN[count][offset][0])):
                for t in range(TILES[count]):
                    places[count, offset, k, t] = at
                    at += height[count]
    return places, at


X_HEIGHT = {1: N, 2: N, 3: N}
Z_HEIGHT = {1: 16, 2: 8, 3: 4}
ALL = (1, 2, 3)
X_UP = message_places(X_HEIGHT, (1,), ALL)
X_DOWN = message_places(X_HEIGHT, (-1,), ALL)
X_FAR = message_places(X_HEIGHT, (2, -2), (3,))
Z_UP = message_places(Z_HEIGHT, (1,), ALL)
Z_DOWN = message_places(Z_HEIGHT, (-1,), ALL)
Z_UP2 = message_places(Z_HEIGHT, (2,), (3,))
Z_DOWN2 = message_places(Z_HEIGHT, (-2,), (3,))


def pack_kernel(first_ref, last_ref, to_down_ref, to_up_ref):
    lane = lax.broadcasted_iota(jnp.int32, (64, 128), 1)
    down = up = jnp.zeros((64, 128), F32)
    for g in range(4):
        mine = (lane >= 32 * g) & (lane < 32 * g + 32)
        rows = pl.ds(64 * g, 64)
        a, b = first_ref[rows, :], last_ref[rows, :]
        a = pltpu.roll(a, 32 * g, 1) if g else a
        b = pltpu.roll(b, (32 * g + 32) % 128, 1) if (32 * g + 32) % 128 else b
        down = jnp.where(mine, a, down)
        up = jnp.where(mine, b, up)
    to_down_ref[...] = down
    to_up_ref[...] = up


def split_dot(x, selection):
    hi = x.astype(jnp.bfloat16)
    rest = x - hi.astype(F32)
    mid = rest.astype(jnp.bfloat16)
    lo = (rest - mid.astype(F32)).astype(jnp.bfloat16)
    dot = functools.partial(jnp.dot, preferred_element_type=F32)
    return (dot(lo, selection) + dot(mid, selection)) + dot(hi, selection)


def y_level(source, tiles, halo, even, odd, out, low_halo):
    half = tiles // 2
    width = half * 128 + 128
    i = lax.broadcasted_iota(jnp.int32, (256, 256), 0)
    j = lax.broadcasted_iota(jnp.int32, (256, 256), 1)
    pick = (i == 2 * (j % 128) + j // 128).astype(jnp.bfloat16)
    i = lax.broadcasted_iota(jnp.int32, (128, 256), 0)
    j = lax.broadcasted_iota(jnp.int32, (128, 256), 1)
    pick_halo = (i == (2 * (j % 128) + j // 128) % 128).astype(jnp.bfloat16)
    for t in range(half):
        both = split_dot(source(t), pick)
        even[:, pl.ds(128 * t, 128)] = both[:, :128]
        odd[:, pl.ds(128 * t, 128)] = both[:, 128:]
    both = split_dot(halo(), pick_halo)
    even[:, pl.ds(128 * half, 128)] = both[:, :128]
    odd[:, pl.ds(128 * half, 128)] = both[:, 128:]
    chunk = 16
    for r in range(0, 256, chunk):
        rows = pl.ds(r, chunk)
        s, d = even[rows, :width], odd[rows, :width]
        ahead = lambda v: pltpu.roll(v, width - 1, 1)
        behind = lambda v: pltpu.roll(v, 1, 1)
        d = d + ALPHA * (s + ahead(s))
        s = s + BETA * (behind(d) + d)
        d = d + GAMMA * (s + ahead(s))
        s = s + DELTA * (behind(d) + d)
        for t in range(half):
            out[t, rows, :] = s[:, 128 * t : 128 * t + 128] * ZETA
            out[half + t, rows, :] = d[:, 128 * t : 128 * t + 128] * (1.0 / ZETA)
        if low_halo is not None:
            low_halo[rows, :] = s[:, 128 * half :] * ZETA


def put(ref, places, key, value):
    ref[pl.ds(places[key], value.shape[0]), :] = value


def y_kernel(x_ref, above_ref, below_ref, o1, o2, o3, up_ref, down_ref, far_ref, even, odd, halo, halo2, g1, g2, g3):
    lane = lax.broadcasted_iota(jnp.int32, (64, 128), 1)
    for g in range(4):
        a, b = above_ref[...], below_ref[...]
        a = pltpu.roll(a, 128 - 32 * g, 1) if g else a
        b = pltpu.roll(b, 96 - 32 * g, 1) if g < 3 else b
        halo[pl.ds(64 * g, 64), :] = jnp.where(lane < 32, a, jnp.where(lane >= 96, b, 0.0))

    def pair(g):
        return lambda t: jnp.concatenate([g[2 * t], g[2 * t + 1]], axis=1)

    y_level(lambda t: x_ref[:, pl.ds(256 * t, 256)], 8, lambda: halo[...], even, odd, g1, halo2)
    y_level(pair(g1), 4, lambda: halo2[...], even, odd, g2, halo)
    y_level(pair(g2), 2, lambda: halo[...], even, odd, g3, None)

    for count, g, o in ((1, g1, o1), (2, g2, o2), (3, g3, o3)):
        n = own_count(count)
        for t in range(TILES[count]):
            rows = [g[t, pl.ds(x, N, stride=N), :] for x in range(N)]
            level = block_levels(rows, count)
            for k, v in enumerate(sent(level, count, 1)):
                put(up_ref, X_UP[0], (count, 1, k, t), v)
            for k, v in enumerate(sent(level, count, -1)):
                put(down_ref, X_DOWN[0], (count, -1, k, t), v)
            if count == 3:
                for offset in (2, -2):
                    for k, v in enumerate(sent(level, count, offset)):
                        put(far_ref, X_FAR[0], (count, offset, k, t), v)
            for b, band in enumerate(BANDS):
                for i in range(n):
                    o[t, pl.ds((b * n + i) * N, N), :] = level.get(band, i)


def received(count, row, t, height, sources):
    total = None
    for offset, places, ref in sources:
        if not PLAN[count][offset][0]:
            continue

        def line(k, offset=offset, places=places, ref=ref):
            return ref[pl.ds(places[count, offset, k, t], height), :]

        lines = [functools.partial(line, k) for k in range(len(PLAN[count][offset][0]))]
        total = plus(total, added(count, offset, row, lines))
    return total


def x_kernel(i1, i2, i3, up_in, down_in, far_in, o1, o2, o3, up_ref, down_ref, up2_ref, down2_ref, g1, g2, g3):
    near = [(1, X_UP[0], up_in), (-1, X_DOWN[0], down_in)]
    far = [(2, X_FAR[0], far_in), (-2, X_FAR[0], far_in)]
    for count, own, g, o in ((1, i1, g1, o1), (2, i2, g2, o2), (3, i3, g3, o3)):
        n = own_count(count)
        sources = near + far if count == 3 else near
        for t in range(TILES[count]):
            for row in range(2 * n):
                here = (t, pl.ds(row * N, N), slice(None))
                g[here] = plus(own[here], received(count, row, t, N, sources))
            rows = [g[t, pl.ds(z, 2 * n, stride=N), :] for z in range(N)]
            level = block_levels(rows, count)
            for k, v in enumerate(sent(level, count, 1)):
                put(up_ref, Z_UP[0], (count, 1, k, t), v)
            for k, v in enumerate(sent(level, count, -1)):
                put(down_ref, Z_DOWN[0], (count, -1, k, t), v)
            if count == 3:
                for k, v in enumerate(sent(level, count, 2)):
                    put(up2_ref, Z_UP2[0], (count, 2, k, t), v)
                for k, v in enumerate(sent(level, count, -2)):
                    put(down2_ref, Z_DOWN2[0], (count, -2, k, t), v)
            for b, band in enumerate(BANDS):
                for i in range(n):
                    o[t, b * n + i] = level.get(band, i)


def z_kernel(i1, i2, i3, up_in, down_in, up2_in, down2_in, one_ref, two_ref, three_ref, last_ref):
    near = [(1, Z_UP[0], up_in), (-1, Z_DOWN[0], down_in)]
    far = [(2, Z_UP2[0], up2_in), (-2, Z_DOWN2[0], down2_in)]
    for count, g, o in ((1, i1, one_ref), (2, i2, two_ref), (3, i3, three_ref)):
        n = own_count(count)
        sources = near + far if count == 3 else near
        for t in range(TILES[count]):
            hy, tile = divmod(t, TILES[count] // 2)
            lanes = pl.ds(128 * tile, 128)
            for row in range(2 * n):
                hz, z = divmod(row, n)
                value = plus(g[t, row], received(count, row, t, 2 * n, sources))
                for hx in range(2):
                    part = value[hx * n : hx * n + n]
                    band = hz * 4 + hy * 2 + hx
                    if band:
                        o[band - 1, z, :, lanes] = part
                    elif count == 3:
                        last_ref[z, :, lanes] = part


VMEM = pl.BlockSpec(memory_space=pltpu.VMEM)
PARAMS = pltpu.CompilerParams(vmem_limit_bytes=24 * 2**20)


def in_vmem(*shapes):
    return tuple(pltpu.VMEM(shape, F32) for shape in shapes)


def pinned(arrays):
    return [pltpu.with_memory_space_constraint(a, pltpu.VMEM) for a in arrays]


def call(kernel, arrays, out_shape, name, scratch=(), out_specs=None):
    arrays = pinned(arrays)
    return pl.pallas_call(
        kernel,
        out_shape=out_shape,
        in_specs=[VMEM] * len(arrays),
        out_specs=out_specs if out_specs is not None else tuple([VMEM] * len(out_shape)),
        scratch_shapes=scratch,
        compiler_params=PARAMS,
        name=name,
    )(*arrays)


def shift(x, axis, by):
    peers = lax.axis_size(axis)
    return lax.ppermute(x, axis, [(i, (i + by) % peers) for i in range(peers)])


def on_device(density):
    flat = density.reshape(N * N, 1024)
    to_down, to_up = pl.pallas_call(
        pack_kernel,
        grid=(1,),
        out_shape=in_vmem((64, 128), (64, 128)),
        in_specs=[pl.BlockSpec((256, 128), lambda i: (0, 0)), pl.BlockSpec((256, 128), lambda i: (0, 7))],
        out_specs=(VMEM, VMEM),
        compiler_params=PARAMS,
        name="pack_y",
    )(flat, flat)
    above = shift(to_down, "gy", -1)
    below = shift(to_up, "gy", 1)

    rows = {c: 2 * own_count(c) for c in ALL}
    outs = in_vmem(*[(TILES[c], rows[c] * N, 128) for c in ALL], *[(m[1], 128) for m in (X_UP, X_DOWN, X_FAR)])
    scratch = in_vmem((256, 640), (256, 640), (256, 128), (256, 128), *[(TILES[c], 256, 128) for c in ALL])
    a1, a2, a3, up, down, far = call(y_kernel, (flat, above, below), outs, "along_y", scratch)
    up = shift(up, "gx", 1)
    down = shift(down, "gx", -1)
    far = shift(far, "gx", 2)

    outs = in_vmem(
        *[(TILES[c], rows[c], rows[c], 128) for c in ALL], *[(m[1], 128) for m in (Z_UP, Z_DOWN, Z_UP2, Z_DOWN2)]
    )
    scratch = in_vmem(*[(TILES[c], rows[c] * N, 128) for c in ALL])
    b1, b2, b3, up, down, up2, down2 = call(x_kernel, (a1, a2, a3, up, down, far), outs, "along_x", scratch)
    up = shift(up, "gz", 1)
    down = shift(down, "gz", -1)
    up2 = shift(up2, "gz", 2)
    down2 = shift(down2, "gz", -2)

    outs = tuple(
        jax.ShapeDtypeStruct(s, F32) for s in ((7, 8, 8, 512), (7, 4, 4, 256), (7, 2, 2, 128), (2, 2, 128))
    )
    return call(z_kernel, (b1, b2, b3, up, down, up2, down2), outs, "along_z")


def solution(mesh):
    return jax.shard_map(
        on_device,
        mesh=mesh,
        in_specs=(P("gz", "gx", "gy"),),
        out_specs=(
            P(None, "gz", "gx", "gy"),
            P(None, "gz", "gx", "gy"),
            P(None, "gz", "gx", "gy"),
            P("gz", "gx", "gy"),
        ),
        check_vma=False,
    )
```

```python
import functools

import jax
import jax.numpy as jnp
import numpy as np
from jax import lax
from jax.experimental import pallas as pl
from jax.experimental.pallas import tpu as pltpu
from jax.sharding import PartitionSpec as P

ALPHA = -1.586134342
BETA = -0.05298011854
GAMMA = 0.8829110762
DELTA = 0.4435068522
ZETA = 1.149604398

N = 16
F32 = jnp.float32


def plus(a, b):
    if a is None:
        return b
    return a if b is None else a + b


def times(c, a):
    return None if a is None else c * a


class Level:
    def __init__(self, line):
        self.line = line
        self.memo = {}

    def get(self, name, i):
        if (name, i) not in self.memo:
            self.memo[name, i] = getattr(self, name)(i)
        return self.memo[name, i]

    def s0(self, i):
        return self.line(2 * i)

    def d0(self, i):
        return self.line(2 * i + 1)

    def d1(self, i):
        return plus(self.get("d0", i), times(ALPHA, plus(self.get("s0", i), self.get("s0", i + 1))))

    def s1(self, i):
        return plus(self.get("s0", i), times(BETA, plus(self.get("d1", i - 1), self.get("d1", i))))

    def d2(self, i):
        return plus(self.get("d1", i), times(GAMMA, plus(self.get("s1", i), self.get("s1", i + 1))))

    def s2(self, i):
        return plus(self.get("s1", i), times(DELTA, plus(self.get("d2", i - 1), self.get("d2", i))))

    def low(self, i):
        return times(ZETA, self.get("s2", i))

    def high(self, i):
        return times(1.0 / ZETA, self.get("d2", i))


def block_levels(rows, count):
    line = lambda i: rows[i] if 0 <= i < N else None
    for _ in range(count):
        level = Level(line)
        line = functools.partial(level.get, "low")
    return level


BANDS = ("low", "high")


def own_count(count):
    return N >> count


def spill_matrices(count):
    n = own_count(count)
    level = block_levels(list(np.eye(N)), count)
    zero = np.zeros(N)

    def at(band, i):
        value = level.get(band, i)
        return zero if value is None else value

    return {
        offset: np.stack([at(band, offset * n + i) for band in BANDS for i in range(n)])
        for offset in (-2, -1, 1, 2)
    }


def factor(matrix):
    picked, rest = [], matrix.copy()
    scale = np.abs(matrix).max()
    while scale > 0 and np.abs(rest).max() > 1e-10 * scale:
        row = int(np.argmax((rest**2).sum(1)))
        picked.append(row)
        q = rest[row] / np.linalg.norm(rest[row])
        rest = rest - np.outer(rest @ q, q)
    picked.sort()
    if not picked:
        return [], None
    coefs = np.linalg.lstsq(matrix[picked].T, matrix.T, rcond=None)[0].T
    coefs[np.abs(coefs) < 1e-9] = 0.0
    coefs[np.abs(coefs - 1.0) < 1e-9] = 1.0
    return picked, coefs


PLAN = {count: {o: factor(m) for o, m in spill_matrices(count).items()} for count in (1, 2, 3)}
TILES = {1: 8, 2: 4, 3: 2}


def sent(level, count, offset):
    n = own_count(count)
    return [level.get(BANDS[row // n], offset * n + row % n) for row in PLAN[count][offset][0]]


def added(count, offset, row, lines):
    coefs = PLAN[count][offset][1][row]
    total = None
    for c, line in zip(coefs, lines):
        if c != 0.0:
            total = plus(total, line() if c == 1.0 else times(float(c), line()))
    return total


def message_places(height, offsets, counts):
    places, at = {}, 0
    for offset in offsets:
        for count in counts:
            for k in range(len(PLAN[count][offset][0])):
                for t in range(TILES[count]):
                    places[count, offset, k, t] = at
                    at += height[count]
    return places, at


X_HEIGHT = {1: N, 2: N, 3: N}
Z_HEIGHT = {1: 16, 2: 8, 3: 4}
ALL = (1, 2, 3)
X_UP = message_places(X_HEIGHT, (1,), ALL)
X_DOWN = message_places(X_HEIGHT, (-1,), ALL)
X_FAR = message_places(X_HEIGHT, (2, -2), (3,))
Z_UP = message_places(Z_HEIGHT, (1,), ALL)
Z_DOWN = message_places(Z_HEIGHT, (-1,), ALL)
Z_UP2 = message_places(Z_HEIGHT, (2,), (3,))
Z_DOWN2 = message_places(Z_HEIGHT, (-2,), (3,))


def pack_kernel(first_ref, last_ref, to_down_ref, to_up_ref):
    lane = lax.broadcasted_iota(jnp.int32, (64, 128), 1)
    down = up = jnp.zeros((64, 128), F32)
    for g in range(4):
        mine = (lane >= 32 * g) & (lane < 32 * g + 32)
        rows = pl.ds(64 * g, 64)
        a, b = first_ref[rows, :], last_ref[rows, :]
        a = pltpu.roll(a, 32 * g, 1) if g else a
        b = pltpu.roll(b, (32 * g + 32) % 128, 1) if (32 * g + 32) % 128 else b
        down = jnp.where(mine, a, down)
        up = jnp.where(mine, b, up)
    to_down_ref[...] = down
    to_up_ref[...] = up


def split_dot(x, selection):
    hi = x.astype(jnp.bfloat16)
    rest = x - hi.astype(F32)
    mid = rest.astype(jnp.bfloat16)
    lo = (rest - mid.astype(F32)).astype(jnp.bfloat16)
    dot = functools.partial(jnp.dot, preferred_element_type=F32)
    return (dot(lo, selection) + dot(mid, selection)) + dot(hi, selection)


def y_level(source, tiles, halo, even, odd, out, low_halo):
    half = tiles // 2
    width = half * 128 + 128
    i = lax.broadcasted_iota(jnp.int32, (256, 256), 0)
    j = lax.broadcasted_iota(jnp.int32, (256, 256), 1)
    pick = (i == 2 * (j % 128) + j // 128).astype(jnp.bfloat16)
    for t in range(half):
        both = split_dot(source(t), pick)
        even[:, pl.ds(128 * t, 128)] = both[:, :128]
        odd[:, pl.ds(128 * t, 128)] = both[:, 128:]
    if halo is None:
        both = jnp.zeros((256, 256), F32)
    else:
        i = lax.broadcasted_iota(jnp.int32, (128, 256), 0)
        j = lax.broadcasted_iota(jnp.int32, (128, 256), 1)
        pick_halo = (i == (2 * (j % 128) + j // 128) % 128).astype(jnp.bfloat16)
        both = split_dot(halo[...], pick_halo)
    even[:, pl.ds(128 * half, 128)] = both[:, :128]
    odd[:, pl.ds(128 * half, 128)] = both[:, 128:]
    chunk = 16
    for r in range(0, 256, chunk):
        rows = pl.ds(r, chunk)
        s, d = even[rows, :width], odd[rows, :width]
        ahead = lambda v: pltpu.roll(v, width - 1, 1)
        behind = lambda v: pltpu.roll(v, 1, 1)
        d = d + ALPHA * (s + ahead(s))
        s = s + BETA * (behind(d) + d)
        d = d + GAMMA * (s + ahead(s))
        s = s + DELTA * (behind(d) + d)
        for t in range(half):
            out[t, rows, :] = s[:, 128 * t : 128 * t + 128] * ZETA
            out[half + t, rows, :] = d[:, 128 * t : 128 * t + 128] * (1.0 / ZETA)
        if low_halo is not None:
            low_halo[rows, :] = s[:, 128 * half :] * ZETA


def put(ref, places, key, value):
    ref[pl.ds(places[key], value.shape[0]), :] = value


def x_lines(g, x):
    return g[pl.ds(x, N, stride=N), :]


def x_spill(level, count):
    for message, offset in ((0, 1), (1, -1)) + (((2, 2), (2, -2)) if count == 3 else ()):
        for k, v in enumerate(sent(level, count, offset)):
            yield message, (count, offset, k), v


X_PLACES = (X_UP[0], X_DOWN[0], X_FAR[0])


def bulk_kernel(x_ref, g1, g2, g3, up_ref, down_ref, far_ref, even, odd, halo1, halo2):
    def pair(g):
        return lambda t: jnp.concatenate([g[2 * t], g[2 * t + 1]], axis=1)

    y_level(lambda t: x_ref[:, pl.ds(256 * t, 256)], 8, None, even, odd, g1, halo1)
    y_level(pair(g1), 4, halo1, even, odd, g2, halo2)
    y_level(pair(g2), 2, halo2, even, odd, g3, None)
    refs = (up_ref, down_ref, far_ref)
    for count, g in ((1, g1), (2, g2), (3, g3)):
        for t in range(TILES[count]):
            level = block_levels([x_lines(g.at[t], x) for x in range(N)], count)
            for m, key, v in x_spill(level, count):
                put(refs[m], X_PLACES[m], key + (t,), v)


def halo_matrix():
    cells = np.eye(128)

    def line(i):
        if 1024 <= i < 1056:
            return cells[i - 1024]
        return cells[128 + i] if -32 <= i < 0 else None

    columns = []
    for count in ALL:
        level = Level(line)
        line = functools.partial(level.get, "low")
        n = 1024 >> count
        for band, start in (("low", 0), ("high", n - 32), ("high", 0), ("low", n - 32)):
            values = [level.get(band, start + i) for i in range(32)]
            columns += [np.zeros(128) if v is None else v for v in values]
    return np.stack(columns, axis=1).astype(np.float32)


def edges(count, t, low, high):
    half = TILES[count] // 2
    value, t = (low, t) if t < half else (high, t - half)
    if t not in (0, half - 1):
        return None
    lane = lax.broadcasted_iota(jnp.int32, value.shape, 1)
    keep = lane < 0
    if t == 0:
        keep |= lane < 32
    if t == half - 1:
        keep |= lane >= 96
    return jnp.where(keep, value, 0.0)


def halo_kernel(above_ref, below_ref, w_ref, up_in, down_in, far_in, d_ref, up_ref, down_ref, far_ref, halo):
    lane = lax.broadcasted_iota(jnp.int32, (64, 128), 1)
    for g in range(4):
        a, b = above_ref[...], below_ref[...]
        a = pltpu.roll(a, 128 - 32 * g, 1) if g else a
        b = pltpu.roll(b, 96 - 32 * g, 1) if g < 3 else b
        halo[pl.ds(64 * g, 64), :] = jnp.where(lane < 32, a, jnp.where(lane >= 96, b, 0.0))
    both = jnp.dot(halo[...], w_ref[...], precision=lax.Precision.HIGHEST, preferred_element_type=F32)
    for c in range(3):
        d_ref[c] = both[:, 128 * c : 128 * c + 128]
    ins, refs = (up_in, down_in, far_in), (up_ref, down_ref, far_ref)
    for count in ALL:
        level = block_levels([x_lines(d_ref.at[count - 1], x) for x in range(N)], count)
        for m, key, v in x_spill(level, count):
            turned = pltpu.roll(v, 64, 1)
            for t in range(TILES[count]):
                own = ins[m][pl.ds(X_PLACES[m][key + (t,)], N), :]
                put(refs[m], X_PLACES[m], key + (t,), plus(own, edges(count, t, v, turned)))


def own_x_kernel(g1, g2, g3, d_ref, o1, o2, o3):
    for count, g, o in ((1, g1, o1), (2, g2, o2), (3, g3, o3)):
        n = own_count(count)
        halo = block_levels([x_lines(d_ref.at[count - 1], x) for x in range(N)], count)
        blocks = [block_levels([x_lines(g.at[t], x) for x in range(N)], count) for t in range(TILES[count])]
        for b, band in enumerate(BANDS):
            for i in range(n):
                v = halo.get(band, i)
                turned = pltpu.roll(v, 64, 1)
                for t in range(TILES[count]):
                    o[t, pl.ds((b * n + i) * N, N), :] = plus(blocks[t].get(band, i), edges(count, t, v, turned))


def received(count, row, t, height, sources):
    total = None
    for offset, places, ref in sources:
        if not PLAN[count][offset][0]:
            continue

        def line(k, offset=offset, places=places, ref=ref):
            return ref[pl.ds(places[count, offset, k, t], height), :]

        lines = [functools.partial(line, k) for k in range(len(PLAN[count][offset][0]))]
        total = plus(total, added(count, offset, row, lines))
    return total


def z_lines(g, t, count):
    return [g[t, pl.ds(z, 2 * own_count(count), stride=N), :] for z in range(N)]


def x_kernel(i1, i2, i3, up_in, down_in, far_in, o1, o2, o3, up_ref, down_ref, up2_ref, down2_ref):
    near = [(1, X_UP[0], up_in), (-1, X_DOWN[0], down_in)]
    far = [(2, X_FAR[0], far_in), (-2, X_FAR[0], far_in)]
    for count, own, g in ((1, i1, o1), (2, i2, o2), (3, i3, o3)):
        n = own_count(count)
        sources = near + far if count == 3 else near
        for t in range(TILES[count]):
            for row in range(2 * n):
                here = (t, pl.ds(row * N, N), slice(None))
                g[here] = plus(own[here], received(count, row, t, N, sources))
            level = block_levels(z_lines(g, t, count), count)
            for k, v in enumerate(sent(level, count, 1)):
                put(up_ref, Z_UP[0], (count, 1, k, t), v)
            for k, v in enumerate(sent(level, count, -1)):
                put(down_ref, Z_DOWN[0], (count, -1, k, t), v)
            if count == 3:
                for k, v in enumerate(sent(level, count, 2)):
                    put(up2_ref, Z_UP2[0], (count, 2, k, t), v)
                for k, v in enumerate(sent(level, count, -2)):
                    put(down2_ref, Z_DOWN2[0], (count, -2, k, t), v)


def own_z_kernel(g1, g2, g3, o1, o2, o3):
    for count, g, o in ((1, g1, o1), (2, g2, o2), (3, g3, o3)):
        n = own_count(count)
        for t in range(TILES[count]):
            level = block_levels(z_lines(g, t, count), count)
            for b, band in enumerate(BANDS):
                for i in range(n):
                    o[t, b * n + i] = level.get(band, i)


def z_kernel(i1, i2, i3, up_in, down_in, up2_in, down2_in, one_ref, two_ref, three_ref, last_ref):
    near = [(1, Z_UP[0], up_in), (-1, Z_DOWN[0], down_in)]
    far = [(2, Z_UP2[0], up2_in), (-2, Z_DOWN2[0], down2_in)]
    for count, g, o in ((1, i1, one_ref), (2, i2, two_ref), (3, i3, three_ref)):
        n = own_count(count)
        sources = near + far if count == 3 else near
        for t in range(TILES[count]):
            hy, tile = divmod(t, TILES[count] // 2)
            lanes = pl.ds(128 * tile, 128)
            for row in range(2 * n):
                hz, z = divmod(row, n)
                value = plus(g[t, row], received(count, row, t, 2 * n, sources))
                for hx in range(2):
                    part = value[hx * n : hx * n + n]
                    band = hz * 4 + hy * 2 + hx
                    if band:
                        o[band - 1, z, :, lanes] = part
                    elif count == 3:
                        last_ref[z, :, lanes] = part


VMEM = pl.BlockSpec(memory_space=pltpu.VMEM)
PARAMS = pltpu.CompilerParams(vmem_limit_bytes=24 * 2**20)


def in_vmem(*shapes):
    return tuple(pltpu.VMEM(shape, F32) for shape in shapes)


def pinned(arrays, space=pltpu.VMEM):
    return [pltpu.with_memory_space_constraint(a, space) for a in arrays]


def call(kernel, arrays, out_shape, name, scratch=(), moved=4):
    arrays = pinned(arrays)
    return pl.pallas_call(
        kernel,
        out_shape=out_shape,
        in_specs=[VMEM] * len(arrays),
        out_specs=tuple([VMEM] * len(out_shape)),
        scratch_shapes=scratch,
        compiler_params=PARAMS,
        cost_estimate=pl.CostEstimate(flops=0, transcendentals=0, bytes_accessed=moved * 2**20),
        name=name,
    )(*arrays)


def shift(x, axis, by):
    peers = lax.axis_size(axis)
    return lax.ppermute(x, axis, [(i, (i + by) % peers) for i in range(peers)])


def on_device(density):
    flat = density.reshape(N * N, 1024)
    in_hbm = pinned([flat], pltpu.HBM)[0]
    to_down, to_up = pl.pallas_call(
        pack_kernel,
        grid=(1,),
        out_shape=in_vmem((64, 128), (64, 128)),
        in_specs=[pl.BlockSpec((256, 128), lambda i: (0, 0)), pl.BlockSpec((256, 128), lambda i: (0, 7))],
        out_specs=(VMEM, VMEM),
        compiler_params=PARAMS,
        name="pack_y",
    )(in_hbm, in_hbm)
    above = shift(to_down, "gy", -1)
    below = shift(to_up, "gy", 1)

    rows = {c: 2 * own_count(c) for c in ALL}
    messages = in_vmem(*[(m[1], 128) for m in (X_UP, X_DOWN, X_FAR)])
    outs = in_vmem(*[(TILES[c], 256, 128) for c in ALL]) + messages
    scratch = in_vmem((256, 640), (256, 640), (256, 128), (256, 128))
    g1, g2, g3, up, down, far = call(bulk_kernel, (flat,), outs, "own_y", scratch, 12)
    outs = in_vmem((3, 256, 128)) + messages
    weights = jnp.asarray(halo_matrix())
    d, up, down, far = call(
        halo_kernel, (above, below, weights, up, down, far), outs, "halo_y", in_vmem((256, 128))
    )
    up = shift(up, "gx", 1)
    down = shift(down, "gx", -1)
    far = shift(far, "gx", 2)

    blocks = in_vmem(*[(TILES[c], rows[c] * N, 128) for c in ALL])
    own = call(own_x_kernel, (g1, g2, g3, d), blocks, "own_x", (), 8)
    outs = blocks + in_vmem(*[(m[1], 128) for m in (Z_UP, Z_DOWN, Z_UP2, Z_DOWN2)])
    a1, a2, a3, up, down, up2, down2 = call(x_kernel, (*own, up, down, far), outs, "spill_x")
    up = shift(up, "gz", 1)
    down = shift(down, "gz", -1)
    up2 = shift(up2, "gz", 2)
    down2 = shift(down2, "gz", -2)

    outs = in_vmem(*[(TILES[c], rows[c], rows[c], 128) for c in ALL])
    own = call(own_z_kernel, (a1, a2, a3), outs, "own_z", (), 8)
    outs = tuple(
        jax.ShapeDtypeStruct(s, F32) for s in ((7, 8, 8, 512), (7, 4, 4, 256), (7, 2, 2, 128), (2, 2, 128))
    )
    return call(z_kernel, (*own, up, down, up2, down2), outs, "spill_z")


def solution(mesh):
    return jax.shard_map(
        on_device,
        mesh=mesh,
        in_specs=(P("gz", "gx", "gy"),),
        out_specs=(
            P(None, "gz", "gx", "gy"),
            P(None, "gz", "gx", "gy"),
            P(None, "gz", "gx", "gy"),
            P("gz", "gx", "gy"),
        ),
        check_vma=False,
    )
```

```python
import functools

import jax
import jax.numpy as jnp
import numpy as np
from jax import lax
from jax.experimental import pallas as pl
from jax.experimental.pallas import tpu as pltpu
from jax.sharding import PartitionSpec as P

ALPHA = -1.586134342
BETA = -0.05298011854
GAMMA = 0.8829110762
DELTA = 0.4435068522
ZETA = 1.149604398

N = 16
F32 = jnp.float32


def plus(a, b):
    if a is None:
        return b
    return a if b is None else a + b


def times(c, a):
    return None if a is None else c * a


class Level:
    def __init__(self, line):
        self.line = line
        self.memo = {}

    def get(self, name, i):
        if (name, i) not in self.memo:
            self.memo[name, i] = getattr(self, name)(i)
        return self.memo[name, i]

    def s0(self, i):
        return self.line(2 * i)

    def d0(self, i):
        return self.line(2 * i + 1)

    def d1(self, i):
        return plus(self.get("d0", i), times(ALPHA, plus(self.get("s0", i), self.get("s0", i + 1))))

    def s1(self, i):
        return plus(self.get("s0", i), times(BETA, plus(self.get("d1", i - 1), self.get("d1", i))))

    def d2(self, i):
        return plus(self.get("d1", i), times(GAMMA, plus(self.get("s1", i), self.get("s1", i + 1))))

    def s2(self, i):
        return plus(self.get("s1", i), times(DELTA, plus(self.get("d2", i - 1), self.get("d2", i))))

    def low(self, i):
        return times(ZETA, self.get("s2", i))

    def high(self, i):
        return times(1.0 / ZETA, self.get("d2", i))


def block_levels(rows, count):
    line = lambda i: rows[i] if 0 <= i < N else None
    for _ in range(count):
        level = Level(line)
        line = functools.partial(level.get, "low")
    return level


BANDS = ("low", "high")


def own_count(count):
    return N >> count


def spill_matrices(count):
    n = own_count(count)
    level = block_levels(list(np.eye(N)), count)
    zero = np.zeros(N)

    def at(band, i):
        value = level.get(band, i)
        return zero if value is None else value

    return {
        offset: np.stack([at(band, offset * n + i) for band in BANDS for i in range(n)])
        for offset in (-2, -1, 1, 2)
    }


def factor(matrix):
    picked, rest = [], matrix.copy()
    scale = np.abs(matrix).max()
    while scale > 0 and np.abs(rest).max() > 1e-10 * scale:
        row = int(np.argmax((rest**2).sum(1)))
        picked.append(row)
        q = rest[row] / np.linalg.norm(rest[row])
        rest = rest - np.outer(rest @ q, q)
    picked.sort()
    if not picked:
        return [], None
    coefs = np.linalg.lstsq(matrix[picked].T, matrix.T, rcond=None)[0].T
    coefs[np.abs(coefs) < 1e-9] = 0.0
    coefs[np.abs(coefs - 1.0) < 1e-9] = 1.0
    return picked, coefs


PLAN = {count: {o: factor(m) for o, m in spill_matrices(count).items()} for count in (1, 2, 3)}
TILES = {1: 8, 2: 4, 3: 2}


def sent(level, count, offset):
    n = own_count(count)
    return [level.get(BANDS[row // n], offset * n + row % n) for row in PLAN[count][offset][0]]


def added(count, offset, row, lines):
    coefs = PLAN[count][offset][1][row]
    total = None
    for c, line in zip(coefs, lines):
        if c != 0.0:
            total = plus(total, line() if c == 1.0 else times(float(c), line()))
    return total


def message_places(height, offsets, counts):
    places, at = {}, 0
    for offset in offsets:
        for count in counts:
            for k in range(len(PLAN[count][offset][0])):
                for t in range(TILES[count]):
                    places[count, offset, k, t] = at
                    at += height[count]
    return places, at


X_HEIGHT = {1: N, 2: N, 3: N}
Z_HEIGHT = {1: 16, 2: 8, 3: 4}
ALL = (1, 2, 3)
X_NEAR = message_places(X_HEIGHT, (1,), ALL)
X_FAR = message_places(X_HEIGHT, (2, -2), (3,))
Z_UP = message_places(Z_HEIGHT, (1,), ALL)
Z_DOWN = message_places(Z_HEIGHT, (-1,), ALL)
Z_UP2 = message_places(Z_HEIGHT, (2,), (3,))
Z_DOWN2 = message_places(Z_HEIGHT, (-2,), (3,))


def pack_kernel(first_ref, last_ref, to_down_ref, to_up_ref):
    lane = lax.broadcasted_iota(jnp.int32, (64, 128), 1)
    down = up = jnp.zeros((64, 128), F32)
    for g in range(4):
        mine = (lane >= 32 * g) & (lane < 32 * g + 32)
        rows = pl.ds(64 * g, 64)
        a, b = first_ref[rows, :], last_ref[rows, :]
        a = pltpu.roll(a, 32 * g, 1) if g else a
        b = pltpu.roll(b, (32 * g + 32) % 128, 1) if (32 * g + 32) % 128 else b
        down = jnp.where(mine, a, down)
        up = jnp.where(mine, b, up)
    to_down_ref[...] = down
    to_up_ref[...] = up


def split_dot(x, selection):
    hi = x.astype(jnp.bfloat16)
    rest = x - hi.astype(F32)
    mid = rest.astype(jnp.bfloat16)
    lo = (rest - mid.astype(F32)).astype(jnp.bfloat16)
    dot = functools.partial(jnp.dot, preferred_element_type=F32)
    return (dot(lo, selection) + dot(mid, selection)) + dot(hi, selection)


def y_level(source, tiles, halo, even, odd, out, low_halo):
    half = tiles // 2
    width = half * 128 + 128
    i = lax.broadcasted_iota(jnp.int32, (256, 256), 0)
    j = lax.broadcasted_iota(jnp.int32, (256, 256), 1)
    pick = (i == 2 * (j % 128) + j // 128).astype(jnp.bfloat16)
    for t in range(half):
        both = split_dot(source(t), pick)
        even[:, pl.ds(128 * t, 128)] = both[:, :128]
        odd[:, pl.ds(128 * t, 128)] = both[:, 128:]
    if halo is None:
        both = jnp.zeros((256, 256), F32)
    else:
        i = lax.broadcasted_iota(jnp.int32, (128, 256), 0)
        j = lax.broadcasted_iota(jnp.int32, (128, 256), 1)
        pick_halo = (i == (2 * (j % 128) + j // 128) % 128).astype(jnp.bfloat16)
        both = split_dot(halo[...], pick_halo)
    even[:, pl.ds(128 * half, 128)] = both[:, :128]
    odd[:, pl.ds(128 * half, 128)] = both[:, 128:]
    chunk = 16
    for r in range(0, 256, chunk):
        rows = pl.ds(r, chunk)
        s, d = even[rows, :width], odd[rows, :width]
        ahead = lambda v: pltpu.roll(v, width - 1, 1)
        behind = lambda v: pltpu.roll(v, 1, 1)
        d = d + ALPHA * (s + ahead(s))
        s = s + BETA * (behind(d) + d)
        d = d + GAMMA * (s + ahead(s))
        s = s + DELTA * (behind(d) + d)
        for t in range(half):
            out[t, rows, :] = s[:, 128 * t : 128 * t + 128] * ZETA
            out[half + t, rows, :] = d[:, 128 * t : 128 * t + 128] * (1.0 / ZETA)
        if low_halo is not None:
            low_halo[rows, :] = s[:, 128 * half :] * ZETA


def put(ref, places, key, value):
    ref[pl.ds(places[key], value.shape[0]), :] = value


def x_lines(g, x):
    return g[pl.ds(x, N, stride=N), :]


def x_near(level, count, even):
    up, down = sent(level, count, 1), sent(level, count, -1)
    for k, v in enumerate(up):
        w = down[k] if k < len(down) else v
        yield (count, 1, k), jnp.where(even, v, w), jnp.where(even, w, v)


def x_far(level, count):
    for offset in (2, -2):
        for k, v in enumerate(sent(level, count, offset)):
            yield (count, offset, k), v


def bulk_kernel(odd_ref, x_ref, g1, g2, g3, chip_ref, across_ref, far_ref, even, odd, halo1, halo2):
    def pair(g):
        return lambda t: jnp.concatenate([g[2 * t], g[2 * t + 1]], axis=1)

    y_level(lambda t: x_ref[:, pl.ds(256 * t, 256)], 8, None, even, odd, g1, halo1)
    y_level(pair(g1), 4, halo1, even, odd, g2, halo2)
    y_level(pair(g2), 2, halo2, even, odd, g3, None)
    for count, g in ((1, g1), (2, g2), (3, g3)):
        for t in range(TILES[count]):
            level = block_levels([x_lines(g.at[t], x) for x in range(N)], count)
            for key, v, w in x_near(level, count, odd_ref[0] == 0):
                put(chip_ref, X_NEAR[0], key + (t,), v)
                put(across_ref, X_NEAR[0], key + (t,), w)
            for key, v in x_far(level, count):
                put(far_ref, X_FAR[0], key + (t,), v)


def halo_matrix():
    cells = np.eye(128)

    def line(i):
        if 1024 <= i < 1056:
            return cells[i - 1024]
        return cells[128 + i] if -32 <= i < 0 else None

    columns = []
    for count in ALL:
        level = Level(line)
        line = functools.partial(level.get, "low")
        n = 1024 >> count
        for band, start in (("low", 0), ("high", n - 32), ("high", 0), ("low", n - 32)):
            values = [level.get(band, start + i) for i in range(32)]
            columns += [np.zeros(128) if v is None else v for v in values]
    return np.stack(columns, axis=1).astype(np.float32)


def edges(count, t, low, high):
    half = TILES[count] // 2
    value, t = (low, t) if t < half else (high, t - half)
    if t not in (0, half - 1):
        return None
    lane = lax.broadcasted_iota(jnp.int32, value.shape, 1)
    keep = lane < 0
    if t == 0:
        keep |= lane < 32
    if t == half - 1:
        keep |= lane >= 96
    return jnp.where(keep, value, 0.0)


def add_edges(out, ins, places, key, value):
    turned = pltpu.roll(value, 64, 1)
    for t in range(TILES[key[0]]):
        own = ins[pl.ds(places[key + (t,)], N), :]
        put(out, places, key + (t,), plus(own, edges(key[0], t, value, turned)))


EDGE = {key: N * at for at, key in enumerate(sorted({key[:3] for key in X_NEAR[0]}))}


def halo_kernel(odd_ref, above_ref, below_ref, w_ref, chip_in, far_in, d_ref, chip_ref, edge_ref, far_ref, halo):
    lane = lax.broadcasted_iota(jnp.int32, (64, 128), 1)
    for g in range(4):
        a, b = above_ref[...], below_ref[...]
        a = pltpu.roll(a, 128 - 32 * g, 1) if g else a
        b = pltpu.roll(b, 96 - 32 * g, 1) if g < 3 else b
        halo[pl.ds(64 * g, 64), :] = jnp.where(lane < 32, a, jnp.where(lane >= 96, b, 0.0))
    both = jnp.dot(halo[...], w_ref[...], precision=lax.Precision.HIGHEST, preferred_element_type=F32)
    for c in range(3):
        d_ref[c] = both[:, 128 * c : 128 * c + 128]
    for count in ALL:
        level = block_levels([x_lines(d_ref.at[count - 1], x) for x in range(N)], count)
        for key, v, w in x_near(level, count, odd_ref[0] == 0):
            add_edges(chip_ref, chip_in, X_NEAR[0], key, v)
            edge_ref[pl.ds(EDGE[key], N), :] = w
        for key, v in x_far(level, count):
            add_edges(far_ref, far_in, X_FAR[0], key, v)


def own_x_kernel(g1, g2, g3, d_ref, o1, o2, o3):
    for count, g, o in ((1, g1, o1), (2, g2, o2), (3, g3, o3)):
        n = own_count(count)
        halo = block_levels([x_lines(d_ref.at[count - 1], x) for x in range(N)], count)
        blocks = [block_levels([x_lines(g.at[t], x) for x in range(N)], count) for t in range(TILES[count])]
        for b, band in enumerate(BANDS):
            for i in range(n):
                v = halo.get(band, i)
                turned = pltpu.roll(v, 64, 1)
                for t in range(TILES[count]):
                    o[t, pl.ds((b * n + i) * N, N), :] = plus(blocks[t].get(band, i), edges(count, t, v, turned))


def received(count, row, t, height, sources):
    total = None
    for offset, places, ref in sources:
        if not PLAN[count][offset][0]:
            continue

        def line(k, offset=offset, places=places, ref=ref):
            return ref(pl.ds(places[count, offset, k, t], height))

        lines = [functools.partial(line, k) for k in range(len(PLAN[count][offset][0]))]
        total = plus(total, added(count, offset, row, lines))
    return total


def z_lines(g, t, count):
    return [g[t, pl.ds(z, 2 * own_count(count), stride=N), :] for z in range(N)]


def rows_of(ref):
    return lambda rows: ref[rows, :]


def x_kernel(
    odd_ref, i1, i2, i3, chip_in, across_in, edge_in, far_in, o1, o2, o3, up_ref, down_ref, up2_ref, down2_ref, below, above
):
    even = odd_ref[0] == 0
    for key, at in EDGE.items():
        line = edge_in[pl.ds(at, N), :]
        turned = pltpu.roll(line, 64, 1)
        for t in range(TILES[key[0]]):
            rows = pl.ds(X_NEAR[0][key + (t,)], N)
            across = plus(across_in[rows, :], edges(key[0], t, line, turned))
            chip = chip_in[rows, :]
            below[rows, :] = jnp.where(even, across, chip)
            above[rows, :] = jnp.where(even, chip, across)
    places = {**X_NEAR[0], **{(c, -1, k, t): at for (c, _, k, t), at in X_NEAR[0].items()}}
    near = [(1, places, rows_of(below)), (-1, places, rows_of(above))]
    far = [(2, X_FAR[0], rows_of(far_in)), (-2, X_FAR[0], rows_of(far_in))]
    for count, own, g in ((1, i1, o1), (2, i2, o2), (3, i3, o3)):
        n = own_count(count)
        sources = near + far if count == 3 else near
        for t in range(TILES[count]):
            for row in range(2 * n):
                here = (t, pl.ds(row * N, N), slice(None))
                g[here] = plus(own[here], received(count, row, t, N, sources))
            level = block_levels(z_lines(g, t, count), count)
            for k, v in enumerate(sent(level, count, 1)):
                put(up_ref, Z_UP[0], (count, 1, k, t), v)
            for k, v in enumerate(sent(level, count, -1)):
                put(down_ref, Z_DOWN[0], (count, -1, k, t), v)
            if count == 3:
                for k, v in enumerate(sent(level, count, 2)):
                    put(up2_ref, Z_UP2[0], (count, 2, k, t), v)
                for k, v in enumerate(sent(level, count, -2)):
                    put(down2_ref, Z_DOWN2[0], (count, -2, k, t), v)


def own_z_kernel(g1, g2, g3, o1, o2, o3):
    for count, g, o in ((1, g1, o1), (2, g2, o2), (3, g3, o3)):
        n = own_count(count)
        for t in range(TILES[count]):
            level = block_levels(z_lines(g, t, count), count)
            for b, band in enumerate(BANDS):
                for i in range(n):
                    o[t, b * n + i] = level.get(band, i)


def z_kernel(i1, i2, i3, up_in, down_in, up2_in, down2_in, one_hbm, two_hbm, three_hbm, last_hbm, one, two, three, last, sems):
    near = [(1, Z_UP[0], rows_of(up_in)), (-1, Z_DOWN[0], rows_of(down_in))]
    far = [(2, Z_UP2[0], rows_of(up2_in)), (-2, Z_DOWN2[0], rows_of(down2_in))]
    leaving = []

    def leave(source, target):
        copy = pltpu.make_async_copy(source, target, sems.at[len(leaving)])
        copy.start()
        leaving.append(copy)

    for count, g, o, hbm in ((1, i1, one, one_hbm), (2, i2, two, two_hbm), (3, i3, three, three_hbm)):
        n = own_count(count)
        sources = near + far if count == 3 else near
        half = TILES[count] // 2
        for hz in range(2):
            for hy in range(2):
                for t in range(hy * half, hy * half + half):
                    lanes = pl.ds(128 * (t - hy * half), 128)
                    for z in range(n):
                        row = hz * n + z
                        value = plus(g[t, row], received(count, row, t, 2 * n, sources))
                        for hx in range(2):
                            part = value[hx * n : hx * n + n]
                            band = hz * 4 + hy * 2 + hx
                            if band:
                                o[band - 1, z, :, lanes] = part
                            elif count == 3:
                                last[z, :, lanes] = part
                if count == 1:
                    first = max(hz * 4 + hy * 2, 1) - 1
                    bands = pl.ds(first, hz * 4 + hy * 2 + 1 - first)
                    leave(o.at[bands], hbm.at[bands])
        if count > 1:
            leave(o, hbm)
    leave(last, last_hbm)
    for copy in leaving:
        copy.wait()


VMEM = pl.BlockSpec(memory_space=pltpu.VMEM)
PARAMS = pltpu.CompilerParams(vmem_limit_bytes=24 * 2**20)


def in_vmem(*shapes):
    return tuple(pltpu.VMEM(shape, F32) for shape in shapes)


def pinned(arrays, space=pltpu.VMEM):
    return [pltpu.with_memory_space_constraint(a, space) for a in arrays]


def call(kernel, arrays, out_shape, name, scratch=(), moved=4, odd=None):
    arrays = pinned(arrays)
    specs = [VMEM] * len(arrays)
    if odd is not None:
        arrays, specs = [odd, *arrays], [pl.BlockSpec(memory_space=pltpu.SMEM), *specs]
    return pl.pallas_call(
        kernel,
        out_shape=out_shape,
        in_specs=specs,
        out_specs=tuple([VMEM] * len(out_shape)),
        scratch_shapes=scratch,
        compiler_params=PARAMS,
        cost_estimate=pl.CostEstimate(flops=0, transcendentals=0, bytes_accessed=moved * 2**20),
        name=name,
    )(*arrays)


def shift(x, axis, by):
    peers = lax.axis_size(axis)
    return lax.ppermute(x, axis, [(i, (i + by) % peers) for i in range(peers)])


def swap(x, axis, first):
    peers = lax.axis_size(axis)
    pairs = [(i % peers, (i + 1) % peers) for i in range(first, first + peers, 2)]
    return lax.ppermute(x, axis, pairs + [(b, a) for a, b in pairs])


def on_device(density):
    flat = density.reshape(N * N, 1024)
    in_hbm = pinned([flat], pltpu.HBM)[0]
    to_down, to_up = pl.pallas_call(
        pack_kernel,
        grid=(1,),
        out_shape=in_vmem((64, 128), (64, 128)),
        in_specs=[pl.BlockSpec((256, 128), lambda i: (0, 0)), pl.BlockSpec((256, 128), lambda i: (0, 7))],
        out_specs=(VMEM, VMEM),
        compiler_params=PARAMS,
        name="pack_y",
    )(in_hbm, in_hbm)
    above = shift(to_down, "gy", -1)
    below = shift(to_up, "gy", 1)

    rows = {c: 2 * own_count(c) for c in ALL}
    odd = (lax.axis_index("gx") % 2).astype(jnp.int32).reshape(1)
    near, edge, far = in_vmem((X_NEAR[1], 128), (N * len(EDGE), 128), (X_FAR[1], 128))
    outs = in_vmem(*[(TILES[c], 256, 128) for c in ALL]) + (near, near, far)
    scratch = in_vmem((256, 640), (256, 640), (256, 128), (256, 128))
    g1, g2, g3, chip, across, far_own = call(bulk_kernel, (flat,), outs, "own_y", scratch, 12, odd)
    across = swap(across, "gx", 1)
    weights = jnp.asarray(halo_matrix())
    outs = in_vmem((3, 256, 128)) + (near, edge, far)
    d, chip, edge, far = call(
        halo_kernel, (above, below, weights, chip, far_own), outs, "halo_y", in_vmem((256, 128)), 4, odd
    )
    edge = swap(edge, "gx", 1)
    chip = swap(chip, "gx", 0)
    far = shift(far, "gx", 2)

    blocks = in_vmem(*[(TILES[c], rows[c] * N, 128) for c in ALL])
    own = call(own_x_kernel, (g1, g2, g3, d), blocks, "own_x", (), 8)
    outs = blocks + in_vmem(*[(m[1], 128) for m in (Z_UP, Z_DOWN, Z_UP2, Z_DOWN2)])
    a1, a2, a3, up, down, up2, down2 = call(
        x_kernel, (*own, chip, across, edge, far), outs, "spill_x", (near, near), 4, odd
    )
    up = shift(up, "gz", 1)
    down = shift(down, "gz", -1)
    up2 = shift(up2, "gz", 2)
    down2 = shift(down2, "gz", -2)

    outs = in_vmem(*[(TILES[c], rows[c], rows[c], 128) for c in ALL])
    own = call(own_z_kernel, (a1, a2, a3), outs, "own_z", (), 8)
    shapes = ((7, 8, 8, 512), (7, 4, 4, 256), (7, 2, 2, 128), (2, 2, 128))
    return pl.pallas_call(
        z_kernel,
        out_shape=tuple(jax.ShapeDtypeStruct(shape, F32) for shape in shapes),
        in_specs=[VMEM] * 7,
        out_specs=tuple([pl.BlockSpec(memory_space=pltpu.HBM)] * 4),
        scratch_shapes=[*in_vmem(*shapes), pltpu.SemaphoreType.DMA((7,))],
        compiler_params=PARAMS,
        name="spill_z",
    )(*pinned((*own, up, down, up2, down2)))


def solution(mesh):
    return jax.shard_map(
        on_device,
        mesh=mesh,
        in_specs=(P("gz", "gx", "gy"),),
        out_specs=(
            P(None, "gz", "gx", "gy"),
            P(None, "gz", "gx", "gy"),
            P(None, "gz", "gx", "gy"),
            P("gz", "gx", "gy"),
        ),
        check_vma=False,
    )
```

```python
import functools

import jax
import jax.numpy as jnp
import numpy as np
from jax import lax
from jax.experimental import pallas as pl
from jax.experimental.pallas import tpu as pltpu
from jax.sharding import PartitionSpec as P

ALPHA = -1.586134342
BETA = -0.05298011854
GAMMA = 0.8829110762
DELTA = 0.4435068522
ZETA = 1.149604398

N = 16
F32 = jnp.float32


def plus(a, b):
    if a is None:
        return b
    return a if b is None else a + b


def times(c, a):
    return None if a is None else c * a


class Level:
    def __init__(self, line):
        self.line = line
        self.memo = {}

    def get(self, name, i):
        if (name, i) not in self.memo:
            self.memo[name, i] = getattr(self, name)(i)
        return self.memo[name, i]

    def s0(self, i):
        return self.line(2 * i)

    def d0(self, i):
        return self.line(2 * i + 1)

    def d1(self, i):
        return plus(self.get("d0", i), times(ALPHA, plus(self.get("s0", i), self.get("s0", i + 1))))

    def s1(self, i):
        return plus(self.get("s0", i), times(BETA, plus(self.get("d1", i - 1), self.get("d1", i))))

    def d2(self, i):
        return plus(self.get("d1", i), times(GAMMA, plus(self.get("s1", i), self.get("s1", i + 1))))

    def s2(self, i):
        return plus(self.get("s1", i), times(DELTA, plus(self.get("d2", i - 1), self.get("d2", i))))

    def low(self, i):
        return times(ZETA, self.get("s2", i))

    def high(self, i):
        return times(1.0 / ZETA, self.get("d2", i))


def block_levels(rows, count):
    line = lambda i: rows[i] if 0 <= i < N else None
    for _ in range(count):
        level = Level(line)
        line = functools.partial(level.get, "low")
    return level


BANDS = ("low", "high")


def own_count(count):
    return N >> count


def spill_matrices(count):
    n = own_count(count)
    level = block_levels(list(np.eye(N)), count)
    zero = np.zeros(N)

    def at(band, i):
        value = level.get(band, i)
        return zero if value is None else value

    return {
        offset: np.stack([at(band, offset * n + i) for band in BANDS for i in range(n)])
        for offset in (-2, -1, 1, 2)
    }


def factor(matrix):
    picked, rest = [], matrix.copy()
    scale = np.abs(matrix).max()
    while scale > 0 and np.abs(rest).max() > 1e-10 * scale:
        row = int(np.argmax((rest**2).sum(1)))
        picked.append(row)
        q = rest[row] / np.linalg.norm(rest[row])
        rest = rest - np.outer(rest @ q, q)
    picked.sort()
    if not picked:
        return [], None
    coefs = np.linalg.lstsq(matrix[picked].T, matrix.T, rcond=None)[0].T
    coefs[np.abs(coefs) < 1e-9] = 0.0
    coefs[np.abs(coefs - 1.0) < 1e-9] = 1.0
    return picked, coefs


PLAN = {count: {o: factor(m) for o, m in spill_matrices(count).items()} for count in (1, 2, 3)}
TILES = {1: 8, 2: 4, 3: 2}


def sent(level, count, offset):
    n = own_count(count)
    return [level.get(BANDS[row // n], offset * n + row % n) for row in PLAN[count][offset][0]]


def added(count, offset, row, lines):
    coefs = PLAN[count][offset][1][row]
    total = None
    for c, line in zip(coefs, lines):
        if c != 0.0:
            total = plus(total, line() if c == 1.0 else times(float(c), line()))
    return total


def message_places(height, offsets, counts):
    places, at = {}, 0
    for offset in offsets:
        for count in counts:
            for k in range(len(PLAN[count][offset][0])):
                for t in range(TILES[count]):
                    places[count, offset, k, t] = at
                    at += height[count]
    return places, at


X_HEIGHT = {1: N, 2: N, 3: N}
Z_HEIGHT = {1: 16, 2: 8, 3: 4}
ALL = (1, 2, 3)
X_NEAR = message_places(X_HEIGHT, (1,), ALL)
X_FAR = message_places(X_HEIGHT, (2, -2), (3,))
Z_UP = message_places(Z_HEIGHT, (1,), ALL)
Z_DOWN = message_places(Z_HEIGHT, (-1,), ALL)
Z_UP2 = message_places(Z_HEIGHT, (2,), (3,))
Z_DOWN2 = message_places(Z_HEIGHT, (-2,), (3,))


def pack_kernel(first_ref, last_ref, to_down_ref, to_up_ref):
    lane = lax.broadcasted_iota(jnp.int32, (64, 128), 1)
    down = up = jnp.zeros((64, 128), F32)
    for g in range(4):
        mine = (lane >= 32 * g) & (lane < 32 * g + 32)
        rows = pl.ds(64 * g, 64)
        a, b = first_ref[rows, :], last_ref[rows, :]
        a = pltpu.roll(a, 32 * g, 1) if g else a
        b = pltpu.roll(b, (32 * g + 32) % 128, 1) if (32 * g + 32) % 128 else b
        down = jnp.where(mine, a, down)
        up = jnp.where(mine, b, up)
    to_down_ref[...] = down
    to_up_ref[...] = up


def split_dot(x, selection):
    hi = x.astype(jnp.bfloat16)
    rest = x - hi.astype(F32)
    mid = rest.astype(jnp.bfloat16)
    lo = (rest - mid.astype(F32)).astype(jnp.bfloat16)
    dot = functools.partial(jnp.dot, preferred_element_type=F32)
    return (dot(lo, selection) + dot(mid, selection)) + dot(hi, selection)


def y_level(source, tiles, even, odd, out):
    half = tiles // 2
    width = half * 128
    i = lax.broadcasted_iota(jnp.int32, (256, 256), 0)
    j = lax.broadcasted_iota(jnp.int32, (256, 256), 1)
    pick = (i == 2 * (j % 128) + j // 128).astype(jnp.bfloat16)
    for block in range(0, 256, 128):
        rows = pl.ds(block, 128)
        for t in range(half):
            both = split_dot(source(t, rows), pick)
            even[rows, pl.ds(128 * t, 128)] = both[:, :128]
            odd[rows, pl.ds(128 * t, 128)] = both[:, 128:]
        for r in range(block, block + 128, 16):
            rows = pl.ds(r, 16)
            s, d = even[rows, :width], odd[rows, :width]
            ahead = lambda v: pltpu.roll(v, width - 1, 1)
            behind = lambda v: pltpu.roll(v, 1, 1)
            d = d + ALPHA * (s + ahead(s))
            s = s + BETA * (behind(d) + d)
            d = d + GAMMA * (s + ahead(s))
            s = s + DELTA * (behind(d) + d)
            for t in range(half):
                out[t, rows, :] = s[:, 128 * t : 128 * t + 128] * ZETA
                out[half + t, rows, :] = d[:, 128 * t : 128 * t + 128] * (1.0 / ZETA)


def put(ref, places, key, value):
    ref[pl.ds(places[key], value.shape[0]), :] = value


def x_lines(g, x):
    return g[pl.ds(x, N, stride=N), :]


def x_near(level, count, even):
    up, down = sent(level, count, 1), sent(level, count, -1)
    for k, v in enumerate(up):
        w = down[k] if k < len(down) else v
        yield (count, 1, k), jnp.where(even, v, w), jnp.where(even, w, v)


def x_far(level, count):
    for offset in (2, -2):
        for k, v in enumerate(sent(level, count, offset)):
            yield (count, offset, k), v


def bulk_kernel(odd_ref, x_ref, g1, g2, g3, chip_ref, across_ref, far_ref, even, odd):
    def pair(g):
        return lambda t, rows: jnp.concatenate([g[2 * t, rows, :], g[2 * t + 1, rows, :]], axis=1)

    def spill(count, g):
        for t in range(TILES[count]):
            level = block_levels([x_lines(g.at[t], x) for x in range(N)], count)
            for key, v, w in x_near(level, count, odd_ref[0] == 0):
                put(chip_ref, X_NEAR[0], key + (t,), v)
                put(across_ref, X_NEAR[0], key + (t,), w)
            for key, v in x_far(level, count):
                put(far_ref, X_FAR[0], key + (t,), v)

    y_level(lambda t, rows: x_ref[rows, pl.ds(256 * t, 256)], 8, even, odd, g1)
    spill(1, g1)
    y_level(pair(g1), 4, even, odd, g2)
    spill(2, g2)
    y_level(pair(g2), 2, even, odd, g3)
    spill(3, g3)


def halo_matrix():
    cells = np.eye(128)

    def line(i):
        if 1024 <= i < 1056:
            return cells[i - 1024]
        return cells[128 + i] if -32 <= i < 0 else None

    columns = []
    for count in ALL:
        level = Level(line)
        line = functools.partial(level.get, "low")
        n = 1024 >> count
        for band, start in (("low", 0), ("high", n - 32), ("high", 0), ("low", n - 32)):
            values = [level.get(band, start + i) for i in range(32)]
            columns += [np.zeros(128) if v is None else v for v in values]
    return np.stack(columns, axis=1).astype(np.float32)


def edges(count, t, low, high):
    half = TILES[count] // 2
    value, t = (low, t) if t < half else (high, t - half)
    if t not in (0, half - 1):
        return None
    lane = lax.broadcasted_iota(jnp.int32, value.shape, 1)
    keep = lane < 0
    if t == 0:
        keep |= lane < 32
    if t == half - 1:
        keep |= lane >= 96
    return jnp.where(keep, value, 0.0)


def add_edges(out, ins, places, key, value):
    turned = pltpu.roll(value, 64, 1)
    for t in range(TILES[key[0]]):
        own = ins[pl.ds(places[key + (t,)], N), :]
        put(out, places, key + (t,), plus(own, edges(key[0], t, value, turned)))


EDGE = {key: N * at for at, key in enumerate(sorted({key[:3] for key in X_NEAR[0]}))}


def halo_kernel(
    odd_ref, above_ref, below_ref, first_ref, last_ref, w_ref, chip_in, far_in, d_ref, chip_ref, edge_ref, far_ref, halo
):
    lane = lax.broadcasted_iota(jnp.int32, (64, 128), 1)
    for g in range(4):
        a, b = above_ref[...] - first_ref[...], below_ref[...] - last_ref[...]
        a = pltpu.roll(a, 128 - 32 * g, 1) if g else a
        b = pltpu.roll(b, 96 - 32 * g, 1) if g < 3 else b
        halo[pl.ds(64 * g, 64), :] = jnp.where(lane < 32, a, jnp.where(lane >= 96, b, 0.0))
    both = jnp.dot(halo[...], w_ref[...], precision=lax.Precision.HIGHEST, preferred_element_type=F32)
    for c in range(3):
        d_ref[c] = both[:, 128 * c : 128 * c + 128]
    for count in ALL:
        level = block_levels([x_lines(d_ref.at[count - 1], x) for x in range(N)], count)
        for key, v, w in x_near(level, count, odd_ref[0] == 0):
            add_edges(chip_ref, chip_in, X_NEAR[0], key, v)
            edge_ref[pl.ds(EDGE[key], N), :] = w
        for key, v in x_far(level, count):
            add_edges(far_ref, far_in, X_FAR[0], key, v)


def own_x_kernel(g1, g2, g3, d_ref, o1, o2, o3):
    for count, g, o in ((1, g1, o1), (2, g2, o2), (3, g3, o3)):
        n = own_count(count)
        halo = block_levels([x_lines(d_ref.at[count - 1], x) for x in range(N)], count)
        blocks = [block_levels([x_lines(g.at[t], x) for x in range(N)], count) for t in range(TILES[count])]
        for b, band in enumerate(BANDS):
            for i in range(n):
                v = halo.get(band, i)
                turned = pltpu.roll(v, 64, 1)
                for t in range(TILES[count]):
                    o[t, pl.ds((b * n + i) * N, N), :] = plus(blocks[t].get(band, i), edges(count, t, v, turned))


def received(count, row, t, height, sources):
    total = None
    for offset, places, ref in sources:
        if not PLAN[count][offset][0]:
            continue

        def line(k, offset=offset, places=places, ref=ref):
            return ref(pl.ds(places[count, offset, k, t], height))

        lines = [functools.partial(line, k) for k in range(len(PLAN[count][offset][0]))]
        total = plus(total, added(count, offset, row, lines))
    return total


def z_lines(g, t, count):
    return [g[t, pl.ds(z, 2 * own_count(count), stride=N), :] for z in range(N)]


def rows_of(ref):
    return lambda rows: ref[rows, :]


def x_kernel(counts, odd_ref, *refs):
    refs = list(refs)
    take = lambda n: [refs.pop(0) for _ in range(n)]
    ins = take(len(counts))
    chip_in, across_in, edge_in = take(3)
    last = counts == (3,)
    if last:
        far_in, up_in, down_in = take(3)
    outs = take(len(counts))
    up_ref, down_ref = take(2)
    if last:
        up2_ref, down2_ref = take(2)
    below, above = take(2)
    even = odd_ref[0] == 0
    for key, at in EDGE.items():
        if key[0] not in counts:
            continue
        line = edge_in[pl.ds(at, N), :]
        turned = pltpu.roll(line, 64, 1)
        for t in range(TILES[key[0]]):
            rows = pl.ds(X_NEAR[0][key + (t,)], N)
            across = plus(across_in[rows, :], edges(key[0], t, line, turned))
            chip = chip_in[rows, :]
            below[rows, :] = jnp.where(even, across, chip)
            above[rows, :] = jnp.where(even, chip, across)
    places = {**X_NEAR[0], **{(c, -1, k, t): at for (c, _, k, t), at in X_NEAR[0].items()}}
    sources = [(1, places, rows_of(below)), (-1, places, rows_of(above))]
    if last:
        sources += [(2, X_FAR[0], rows_of(far_in)), (-2, X_FAR[0], rows_of(far_in))]
        for taken, ref, message in ((up_in, up_ref, Z_UP), (down_in, down_ref, Z_DOWN)):
            shared = pl.ds(0, min(at for key, at in message[0].items() if key[0] == 3))
            ref[shared, :] = taken[shared, :]
    for count, own, g in zip(counts, ins, outs):
        n = own_count(count)
        for t in range(TILES[count]):
            for row in range(2 * n):
                here = (t, pl.ds(row * N, N), slice(None))
                g[here] = plus(own[here], received(count, row, t, N, sources))
            level = block_levels(z_lines(g, t, count), count)
            for k, v in enumerate(sent(level, count, 1)):
                put(up_ref, Z_UP[0], (count, 1, k, t), v)
            for k, v in enumerate(sent(level, count, -1)):
                put(down_ref, Z_DOWN[0], (count, -1, k, t), v)
            if last:
                for k, v in enumerate(sent(level, count, 2)):
                    put(up2_ref, Z_UP2[0], (count, 2, k, t), v)
                for k, v in enumerate(sent(level, count, -2)):
                    put(down2_ref, Z_DOWN2[0], (count, -2, k, t), v)


def own_z_kernel(g1, g2, g3, o1, o2, o3):
    for count, g, o in ((1, g1, o1), (2, g2, o2), (3, g3, o3)):
        n = own_count(count)
        for t in range(TILES[count]):
            level = block_levels(z_lines(g, t, count), count)
            for b, band in enumerate(BANDS):
                for i in range(n):
                    o[t, b * n + i] = level.get(band, i)


def z_values(count, g, sources):
    n = own_count(count)
    half = TILES[count] // 2
    for hz in range(2):
        for hy in range(2):
            for t in range(hy * half, hy * half + half):
                for z in range(n):
                    row = hz * n + z
                    value = plus(g[t, row], received(count, row, t, 2 * n, sources))
                    for hx in range(2):
                        yield hz * 4 + hy * 2 + hx, z, t - hy * half, value[hx * n : hx * n + n]


def z_near(up_in, down_in):
    return [(1, Z_UP[0], rows_of(up_in)), (-1, Z_DOWN[0], rows_of(down_in))]


def z_kernel(i1, i2, up_in, down_in, one_hbm, two_hbm, one, two, sems):
    leaving = []

    def leave(source, target):
        copy = pltpu.make_async_copy(source, target, sems.at[len(leaving)])
        copy.start()
        leaving.append(copy)

    done = 0
    for band, z, tile, value in z_values(1, i1, z_near(up_in, down_in)):
        if band // 2 != done:
            bands = pl.ds(max(2 * done, 1) - 1, min(2, 2 * done + 1))
            leave(one.at[bands], one_hbm.at[bands])
            done = band // 2
        if band:
            one[band - 1, z, :, pl.ds(128 * tile, 128)] = value
    bands = pl.ds(5, 2)
    leave(one.at[bands], one_hbm.at[bands])
    for band, z, tile, value in z_values(2, i2, z_near(up_in, down_in)):
        if band:
            two[band - 1, z, :, pl.ds(128 * tile, 128)] = value
    leave(two, two_hbm)
    for copy in leaving:
        copy.wait()


def z_last_kernel(i3, up_in, down_in, up2_in, down2_in, three, last):
    far = [(2, Z_UP2[0], rows_of(up2_in)), (-2, Z_DOWN2[0], rows_of(down2_in))]
    for band, z, _, value in z_values(3, i3, z_near(up_in, down_in) + far):
        if band:
            three[band - 1, z] = value
        else:
            last[z] = value


VMEM = pl.BlockSpec(memory_space=pltpu.VMEM)
PARAMS = pltpu.CompilerParams(vmem_limit_bytes=24 * 2**20)


def in_vmem(*shapes):
    return tuple(pltpu.VMEM(shape, F32) for shape in shapes)


def pinned(arrays, space=pltpu.VMEM):
    return [pltpu.with_memory_space_constraint(a, space) for a in arrays]


def call(kernel, arrays, out_shape, name, scratch=(), moved=4, odd=None):
    arrays = pinned(arrays)
    specs = [VMEM] * len(arrays)
    if odd is not None:
        arrays, specs = [odd, *arrays], [pl.BlockSpec(memory_space=pltpu.SMEM), *specs]
    return pl.pallas_call(
        kernel,
        out_shape=out_shape,
        in_specs=specs,
        out_specs=tuple([VMEM] * len(out_shape)),
        scratch_shapes=scratch,
        compiler_params=PARAMS,
        cost_estimate=pl.CostEstimate(flops=0, transcendentals=0, bytes_accessed=moved * 2**20),
        name=name,
    )(*arrays)


def shift(x, axis, by):
    peers = lax.axis_size(axis)
    return lax.ppermute(x, axis, [(i, (i + by) % peers) for i in range(peers)])


def swap(x, axis, first):
    peers = lax.axis_size(axis)
    pairs = [(i % peers, (i + 1) % peers) for i in range(first, first + peers, 2)]
    return lax.ppermute(x, axis, pairs + [(b, a) for a, b in pairs])


def on_device(density):
    flat = density.reshape(N * N, 1024)
    in_hbm = pinned([flat], pltpu.HBM)[0]
    to_down, to_up = pl.pallas_call(
        pack_kernel,
        grid=(1,),
        out_shape=in_vmem((64, 128), (64, 128)),
        in_specs=[pl.BlockSpec((256, 128), lambda i: (0, 0)), pl.BlockSpec((256, 128), lambda i: (0, 7))],
        out_specs=(VMEM, VMEM),
        compiler_params=PARAMS,
        name="pack_y",
    )(in_hbm, in_hbm)
    above = shift(to_down, "gy", -1)
    below = shift(to_up, "gy", 1)

    rows = {c: 2 * own_count(c) for c in ALL}
    odd = (lax.axis_index("gx") % 2).astype(jnp.int32).reshape(1)
    near, edge, far = in_vmem((X_NEAR[1], 128), (N * len(EDGE), 128), (X_FAR[1], 128))
    outs = in_vmem(*[(TILES[c], 256, 128) for c in ALL]) + (near, near, far)
    scratch = in_vmem((256, 512), (256, 512))
    g1, g2, g3, chip, across, far_own = call(bulk_kernel, (flat,), outs, "own_y", scratch, 12, odd)
    across = swap(across, "gx", 1)
    weights = jnp.asarray(halo_matrix())
    outs = in_vmem((3, 256, 128)) + (near, edge, far)
    d, chip, edge, far = call(
        halo_kernel,
        (above, below, to_down, to_up, weights, chip, far_own),
        outs,
        "halo_y",
        in_vmem((256, 128)),
        4,
        odd,
    )
    edge = swap(edge, "gx", 1)
    chip = swap(chip, "gx", 0)
    far = shift(far, "gx", 2)

    blocks = in_vmem(*[(TILES[c], rows[c] * N, 128) for c in ALL])
    own = call(own_x_kernel, (g1, g2, g3, d), blocks, "own_x", (), 8)
    messages = in_vmem(*[(m[1], 128) for m in (Z_UP, Z_DOWN, Z_UP2, Z_DOWN2)])
    near_x = (chip, across, edge)
    a1, a2, up, down = call(
        functools.partial(x_kernel, (1, 2)), (*own[:2], *near_x), blocks[:2] + messages[:2], "spill_x", (near, near), 6, odd
    )
    a3, up, down, up2, down2 = call(
        functools.partial(x_kernel, (3,)),
        (own[2], *near_x, far, up, down),
        blocks[2:] + messages,
        "spill_x_last",
        (near, near),
        1,
        odd,
    )
    up = shift(up, "gz", 1)
    down = shift(down, "gz", -1)
    up2 = shift(up2, "gz", 2)
    down2 = shift(down2, "gz", -2)

    outs = in_vmem(*[(TILES[c], rows[c], rows[c], 128) for c in ALL])
    own = call(own_z_kernel, (a1, a2, a3), outs, "own_z", (), 8)
    shapes = ((7, 8, 8, 512), (7, 4, 4, 256), (7, 2, 2, 128), (2, 2, 128))
    one, two = pl.pallas_call(
        z_kernel,
        out_shape=tuple(jax.ShapeDtypeStruct(shape, F32) for shape in shapes[:2]),
        in_specs=[VMEM] * 4,
        out_specs=tuple([pl.BlockSpec(memory_space=pltpu.HBM)] * 2),
        scratch_shapes=[*in_vmem(*shapes[:2]), pltpu.SemaphoreType.DMA((5,))],
        compiler_params=PARAMS,
        cost_estimate=pl.CostEstimate(flops=0, transcendentals=0, bytes_accessed=6 * 2**20),
        name="spill_z",
    )(*pinned((*own[:2], up, down)))
    outs = tuple(jax.ShapeDtypeStruct(shape, F32) for shape in shapes[2:])
    three, last = call(z_last_kernel, (own[2], up, down, up2, down2), outs, "spill_z_last", (), 1)
    return one, two, three, last


def solution(mesh):
    return jax.shard_map(
        on_device,
        mesh=mesh,
        in_specs=(P("gz", "gx", "gy"),),
        out_specs=(
            P(None, "gz", "gx", "gy"),
            P(None, "gz", "gx", "gy"),
            P(None, "gz", "gx", "gy"),
            P("gz", "gx", "gy"),
        ),
        check_vma=False,
    )
```

```python
import functools

import jax
import jax.numpy as jnp
import numpy as np
from jax import lax
from jax.experimental import pallas as pl
from jax.experimental.pallas import tpu as pltpu
from jax.sharding import PartitionSpec as P

ALPHA = -1.586134342
BETA = -0.05298011854
GAMMA = 0.8829110762
DELTA = 0.4435068522
ZETA = 1.149604398

N = 16
F32 = jnp.float32


def plus(a, b):
    if a is None:
        return b
    return a if b is None else a + b


def times(c, a):
    return None if a is None else c * a


class Level:
    def __init__(self, line):
        self.line = line
        self.memo = {}

    def get(self, name, i):
        if (name, i) not in self.memo:
            self.memo[name, i] = getattr(self, name)(i)
        return self.memo[name, i]

    def s0(self, i):
        return self.line(2 * i)

    def d0(self, i):
        return self.line(2 * i + 1)

    def d1(self, i):
        return plus(self.get("d0", i), times(ALPHA, plus(self.get("s0", i), self.get("s0", i + 1))))

    def s1(self, i):
        return plus(self.get("s0", i), times(BETA, plus(self.get("d1", i - 1), self.get("d1", i))))

    def d2(self, i):
        return plus(self.get("d1", i), times(GAMMA, plus(self.get("s1", i), self.get("s1", i + 1))))

    def s2(self, i):
        return plus(self.get("s1", i), times(DELTA, plus(self.get("d2", i - 1), self.get("d2", i))))

    def low(self, i):
        return times(ZETA, self.get("s2", i))

    def high(self, i):
        return times(1.0 / ZETA, self.get("d2", i))


def block_levels(rows, count):
    line = lambda i: rows[i] if 0 <= i < N else None
    for _ in range(count):
        level = Level(line)
        line = functools.partial(level.get, "low")
    return level


BANDS = ("low", "high")


def own_count(count):
    return N >> count


def spill_matrices(count):
    n = own_count(count)
    level = block_levels(list(np.eye(N)), count)
    zero = np.zeros(N)

    def at(band, i):
        value = level.get(band, i)
        return zero if value is None else value

    return {
        offset: np.stack([at(band, offset * n + i) for band in BANDS for i in range(n)])
        for offset in (-2, -1, 1, 2)
    }


def factor(matrix):
    picked, rest = [], matrix.copy()
    scale = np.abs(matrix).max()
    while scale > 0 and np.abs(rest).max() > 1e-10 * scale:
        row = int(np.argmax((rest**2).sum(1)))
        picked.append(row)
        q = rest[row] / np.linalg.norm(rest[row])
        rest = rest - np.outer(rest @ q, q)
    picked.sort()
    if not picked:
        return [], None
    coefs = np.linalg.lstsq(matrix[picked].T, matrix.T, rcond=None)[0].T
    coefs[np.abs(coefs) < 1e-9] = 0.0
    coefs[np.abs(coefs - 1.0) < 1e-9] = 1.0
    return picked, coefs


PLAN = {count: {o: factor(m) for o, m in spill_matrices(count).items()} for count in (1, 2, 3)}
TILES = {1: 8, 2: 4, 3: 2}


def sent(level, count, offset):
    n = own_count(count)
    return [level.get(BANDS[row // n], offset * n + row % n) for row in PLAN[count][offset][0]]


def added(count, offset, row, lines):
    coefs = PLAN[count][offset][1][row]
    total = None
    for c, line in zip(coefs, lines):
        if c != 0.0:
            total = plus(total, line() if c == 1.0 else times(float(c), line()))
    return total


def message_places(height, offsets, counts):
    places, at = {}, 0
    for offset in offsets:
        for count in counts:
            for k in range(len(PLAN[count][offset][0])):
                for t in range(TILES[count]):
                    places[count, offset, k, t] = at
                    at += height[count]
    return places, at


X_HEIGHT = {1: N, 2: N, 3: N}
Z_HEIGHT = {1: 16, 2: 8, 3: 4}
ALL = (1, 2, 3)
X_NEAR = message_places(X_HEIGHT, (1,), ALL)
X_FAR = message_places(X_HEIGHT, (2, -2), (3,))
Z_UP = message_places(Z_HEIGHT, (1,), ALL)
Z_DOWN = message_places(Z_HEIGHT, (-1,), ALL)
Z_UP2 = message_places(Z_HEIGHT, (2,), (3,))
Z_DOWN2 = message_places(Z_HEIGHT, (-2,), (3,))


def pack_kernel(turn, x_ref, out_ref):
    lane = lax.broadcasted_iota(jnp.int32, (64, 128), 1)
    packed = jnp.zeros((64, 128), F32)
    for g in range(4):
        mine = (lane >= 32 * g) & (lane < 32 * g + 32)
        a = x_ref[pl.ds(64 * g, 64), pl.ds(0 if turn == 0 else x_ref.shape[1] - 128, 128)]
        by = (32 * g + turn) % 128
        packed = jnp.where(mine, pltpu.roll(a, by, 1) if by else a, packed)
    out_ref[:64, :] = packed
    if out_ref.shape[0] > 64:
        out_ref[64:, :] = jnp.zeros((out_ref.shape[0] - 64, 128), F32)


def split_dot(x, selection):
    hi = x.astype(jnp.bfloat16)
    rest = x - hi.astype(F32)
    mid = rest.astype(jnp.bfloat16)
    lo = (rest - mid.astype(F32)).astype(jnp.bfloat16)
    dot = functools.partial(jnp.dot, preferred_element_type=F32)
    return (dot(lo, selection) + dot(mid, selection)) + dot(hi, selection)


def y_level(source, tiles, even, odd, out):
    half = tiles // 2
    width = half * 128
    i = lax.broadcasted_iota(jnp.int32, (256, 256), 0)
    j = lax.broadcasted_iota(jnp.int32, (256, 256), 1)
    pick = (i == 2 * (j % 128) + j // 128).astype(jnp.bfloat16)
    for block in range(0, 256, 128):
        rows = pl.ds(block, 128)
        for t in range(half):
            both = split_dot(source(t, rows), pick)
            even[rows, pl.ds(128 * t, 128)] = both[:, :128]
            odd[rows, pl.ds(128 * t, 128)] = both[:, 128:]
        for r in range(block, block + 128, 64):
            rows = pl.ds(r, 64)
            s, d = even[rows, :width], odd[rows, :width]
            ahead = lambda v: pltpu.roll(v, width - 1, 1)
            behind = lambda v: pltpu.roll(v, 1, 1)
            d = d + ALPHA * (s + ahead(s))
            s = s + BETA * (behind(d) + d)
            d = d + GAMMA * (s + ahead(s))
            s = s + DELTA * (behind(d) + d)
            for t in range(half):
                out[t, rows, :] = s[:, 128 * t : 128 * t + 128] * ZETA
                out[half + t, rows, :] = d[:, 128 * t : 128 * t + 128] * (1.0 / ZETA)


def put(ref, places, key, value):
    ref[pl.ds(places[key], value.shape[0]), :] = value


def x_lines(g, x):
    return g[pl.ds(x, N, stride=N), :]


def x_near(level, count, even):
    up, down = sent(level, count, 1), sent(level, count, -1)
    for k, v in enumerate(up):
        w = down[k] if k < len(down) else v
        yield (count, 1, k), jnp.where(even, v, w), jnp.where(even, w, v)


def x_far(level, count):
    for offset in (2, -2):
        for k, v in enumerate(sent(level, count, offset)):
            yield (count, offset, k), v


def bulk_kernel(odd_ref, x_ref, g1, g2, g3, chip_ref, across_ref, far_ref, even, odd):
    def pair(g):
        return lambda t, rows: jnp.concatenate([g[2 * t, rows, :], g[2 * t + 1, rows, :]], axis=1)

    def spill(count, g):
        for t in range(TILES[count]):
            level = block_levels([x_lines(g.at[t], x) for x in range(N)], count)
            for key, v, w in x_near(level, count, odd_ref[0] == 0):
                put(chip_ref, X_NEAR[0], key + (t,), v)
                put(across_ref, X_NEAR[0], key + (t,), w)
            for key, v in x_far(level, count):
                put(far_ref, X_FAR[0], key + (t,), v)

    y_level(lambda t, rows: x_ref[rows, pl.ds(256 * t, 256)], 8, even, odd, g1)
    spill(1, g1)
    y_level(pair(g1), 4, even, odd, g2)
    spill(2, g2)
    y_level(pair(g2), 2, even, odd, g3)
    spill(3, g3)


def halo_matrix():
    cells = np.eye(128)

    def line(i):
        if 1024 <= i < 1056:
            return cells[i - 1024]
        return cells[128 + i] if -32 <= i < 0 else None

    columns = []
    for count in ALL:
        level = Level(line)
        line = functools.partial(level.get, "low")
        n = 1024 >> count
        for band, start in (("low", 0), ("high", n - 32), ("high", 0), ("low", n - 32)):
            values = [level.get(band, start + i) for i in range(32)]
            columns += [np.zeros(128) if v is None else v for v in values]
    return np.stack(columns, axis=1).astype(np.float32)


def edges(count, t, low, high):
    half = TILES[count] // 2
    value, t = (low, t) if t < half else (high, t - half)
    if t not in (0, half - 1):
        return None
    lane = lax.broadcasted_iota(jnp.int32, value.shape, 1)
    keep = lane < 0
    if t == 0:
        keep |= lane < 32
    if t == half - 1:
        keep |= lane >= 96
    return jnp.where(keep, value, 0.0)


def add_edges(out, ins, places, key, value):
    turned = pltpu.roll(value, 64, 1)
    for t in range(TILES[key[0]]):
        own = ins[pl.ds(places[key + (t,)], N), :]
        put(out, places, key + (t,), plus(own, edges(key[0], t, value, turned)))


EDGE = {key: N * at for at, key in enumerate(sorted({key[:3] for key in X_NEAR[0]}))}


def halo_kernel(
    odd_ref, above_ref, below_ref, first_ref, last_ref, w_ref, chip_in, far_in, d_ref, chip_ref, edge_ref, far_ref, halo
):
    lane = lax.broadcasted_iota(jnp.int32, (64, 128), 1)
    for g in range(4):
        a, b = above_ref[...] - first_ref[...], below_ref[:64, :] - last_ref[:64, :]
        a = pltpu.roll(a, 128 - 32 * g, 1) if g else a
        b = pltpu.roll(b, 96 - 32 * g, 1) if g < 3 else b
        halo[pl.ds(64 * g, 64), :] = jnp.where(lane < 32, a, jnp.where(lane >= 96, b, 0.0))
    both = jnp.dot(halo[...], w_ref[...], precision=lax.Precision.HIGHEST, preferred_element_type=F32)
    for c in range(3):
        d_ref[c] = both[:, 128 * c : 128 * c + 128]
    for count in ALL:
        level = block_levels([x_lines(d_ref.at[count - 1], x) for x in range(N)], count)
        for key, v, w in x_near(level, count, odd_ref[0] == 0):
            add_edges(chip_ref, chip_in, X_NEAR[0], key, v)
            edge_ref[pl.ds(EDGE[key], N), :] = w
        for key, v in x_far(level, count):
            add_edges(far_ref, far_in, X_FAR[0], key, v)


def own_x_kernel(g1, g2, g3, d_ref, o1, o2, o3):
    for count, g, o in ((1, g1, o1), (2, g2, o2), (3, g3, o3)):
        n = own_count(count)
        halo = block_levels([x_lines(d_ref.at[count - 1], x) for x in range(N)], count)
        blocks = [block_levels([x_lines(g.at[t], x) for x in range(N)], count) for t in range(TILES[count])]
        for b, band in enumerate(BANDS):
            for i in range(n):
                v = halo.get(band, i)
                turned = pltpu.roll(v, 64, 1)
                for t in range(TILES[count]):
                    o[t, pl.ds((b * n + i) * N, N), :] = plus(blocks[t].get(band, i), edges(count, t, v, turned))


def received(count, row, t, height, sources):
    total = None
    for offset, places, ref in sources:
        if not PLAN[count][offset][0]:
            continue

        def line(k, offset=offset, places=places, ref=ref):
            return ref(pl.ds(places[count, offset, k, t], height))

        lines = [functools.partial(line, k) for k in range(len(PLAN[count][offset][0]))]
        total = plus(total, added(count, offset, row, lines))
    return total


def z_lines(g, t, count):
    return [g[t, pl.ds(z, 2 * own_count(count), stride=N), :] for z in range(N)]


def rows_of(ref):
    return lambda rows: ref[rows, :]


def x_kernel(counts, odd_ref, *refs):
    refs = list(refs)
    take = lambda n: [refs.pop(0) for _ in range(n)]
    ins = take(len(counts))
    chip_in, across_in, edge_in = take(3)
    last = counts == (3,)
    if last:
        far_in, up_in, down_in = take(3)
    outs = take(len(counts))
    up_ref, down_ref = take(2)
    if last:
        up2_ref, down2_ref = take(2)
    below, above = take(2)
    even = odd_ref[0] == 0
    for key, at in EDGE.items():
        if key[0] not in counts:
            continue
        line = edge_in[pl.ds(at, N), :]
        turned = pltpu.roll(line, 64, 1)
        for t in range(TILES[key[0]]):
            rows = pl.ds(X_NEAR[0][key + (t,)], N)
            across = plus(across_in[rows, :], edges(key[0], t, line, turned))
            chip = chip_in[rows, :]
            below[rows, :] = jnp.where(even, across, chip)
            above[rows, :] = jnp.where(even, chip, across)
    places = {**X_NEAR[0], **{(c, -1, k, t): at for (c, _, k, t), at in X_NEAR[0].items()}}
    sources = [(1, places, rows_of(below)), (-1, places, rows_of(above))]
    if last:
        sources += [(2, X_FAR[0], rows_of(far_in)), (-2, X_FAR[0], rows_of(far_in))]
        for taken, ref, message in ((up_in, up_ref, Z_UP), (down_in, down_ref, Z_DOWN)):
            shared = pl.ds(0, min(at for key, at in message[0].items() if key[0] == 3))
            ref[shared, :] = taken[shared, :]
    for count, own, g in zip(counts, ins, outs):
        n = own_count(count)
        for t in range(TILES[count]):
            for row in range(2 * n):
                here = (t, pl.ds(row * N, N), slice(None))
                g[here] = plus(own[here], received(count, row, t, N, sources))
            level = block_levels(z_lines(g, t, count), count)
            for k, v in enumerate(sent(level, count, 1)):
                put(up_ref, Z_UP[0], (count, 1, k, t), v)
            for k, v in enumerate(sent(level, count, -1)):
                put(down_ref, Z_DOWN[0], (count, -1, k, t), v)
            if last:
                for k, v in enumerate(sent(level, count, 2)):
                    put(up2_ref, Z_UP2[0], (count, 2, k, t), v)
                for k, v in enumerate(sent(level, count, -2)):
                    put(down2_ref, Z_DOWN2[0], (count, -2, k, t), v)


def own_z_kernel(g1, g2, g3, o1, o2, o3):
    for count, g, o in ((1, g1, o1), (2, g2, o2), (3, g3, o3)):
        n = own_count(count)
        for t in range(TILES[count]):
            level = block_levels(z_lines(g, t, count), count)
            for b, band in enumerate(BANDS):
                for i in range(n):
                    o[t, b * n + i] = level.get(band, i)


def z_values(count, g, sources):
    n = own_count(count)
    half = TILES[count] // 2
    for hz in range(2):
        for hy in range(2):
            for t in range(hy * half, hy * half + half):
                for z in range(n):
                    row = hz * n + z
                    value = plus(g[t, row], received(count, row, t, 2 * n, sources))
                    for hx in range(2):
                        yield hz * 4 + hy * 2 + hx, z, t - hy * half, value[hx * n : hx * n + n]


def z_near(up_in, down_in):
    return [(1, Z_UP[0], rows_of(up_in)), (-1, Z_DOWN[0], rows_of(down_in))]


def z_kernel(i1, i2, up_in, down_in, one_hbm, two_hbm, one, two, sems):
    leaving = []

    def leave(source, target):
        copy = pltpu.make_async_copy(source, target, sems.at[len(leaving)])
        copy.start()
        leaving.append(copy)

    done = 0
    for band, z, tile, value in z_values(1, i1, z_near(up_in, down_in)):
        if band // 2 != done:
            bands = pl.ds(max(2 * done, 1) - 1, min(2, 2 * done + 1))
            leave(one.at[bands], one_hbm.at[bands])
            done = band // 2
        if band:
            one[band - 1, z, :, pl.ds(128 * tile, 128)] = value
    bands = pl.ds(5, 2)
    leave(one.at[bands], one_hbm.at[bands])
    for band, z, tile, value in z_values(2, i2, z_near(up_in, down_in)):
        if band:
            two[band - 1, z, :, pl.ds(128 * tile, 128)] = value
    leave(two, two_hbm)
    for copy in leaving:
        copy.wait()


def z_last_kernel(i3, up_in, down_in, up2_in, down2_in, three, last):
    far = [(2, Z_UP2[0], rows_of(up2_in)), (-2, Z_DOWN2[0], rows_of(down2_in))]
    for band, z, _, value in z_values(3, i3, z_near(up_in, down_in) + far):
        if band:
            three[band - 1, z] = value
        else:
            last[z] = value


VMEM = pl.BlockSpec(memory_space=pltpu.VMEM)
PARAMS = pltpu.CompilerParams(vmem_limit_bytes=24 * 2**20)


def in_vmem(*shapes):
    return tuple(pltpu.VMEM(shape, F32) for shape in shapes)


def pinned(arrays, space=pltpu.VMEM):
    return [pltpu.with_memory_space_constraint(a, space) for a in arrays]


def call(kernel, arrays, out_shape, name, scratch=(), moved=4, odd=None):
    arrays = pinned(arrays)
    specs = [VMEM] * len(arrays)
    if odd is not None:
        arrays, specs = [odd, *arrays], [pl.BlockSpec(memory_space=pltpu.SMEM), *specs]
    return pl.pallas_call(
        kernel,
        out_shape=out_shape,
        in_specs=specs,
        out_specs=tuple([VMEM] * len(out_shape)),
        scratch_shapes=scratch,
        compiler_params=PARAMS,
        cost_estimate=pl.CostEstimate(flops=0, transcendentals=0, bytes_accessed=moved * 2**20),
        name=name,
    )(*arrays)


def shift(x, axis, by):
    peers = lax.axis_size(axis)
    return lax.ppermute(x, axis, [(i, (i + by) % peers) for i in range(peers)])


def swap(x, axis, first):
    peers = lax.axis_size(axis)
    pairs = [(i % peers, (i + 1) % peers) for i in range(first, first + peers, 2)]
    return lax.ppermute(x, axis, pairs + [(b, a) for a, b in pairs])


def on_device(density):
    flat = density.reshape(N * N, 1024)
    in_hbm = pinned([flat], pltpu.HBM)[0]
    (to_up,) = pl.pallas_call(
        functools.partial(pack_kernel, 32),
        grid=(1,),
        out_shape=in_vmem((72, 128)),
        in_specs=[pl.BlockSpec((256, 128), lambda i: (0, 7))],
        out_specs=(VMEM,),
        compiler_params=PARAMS,
        name="pack_up",
    )(in_hbm)
    (to_down,) = call(functools.partial(pack_kernel, 0), (flat,), in_vmem((64, 128)), "pack_down", (), 1)
    above = shift(to_down, "gy", -1)
    below = shift(to_up, "gy", 1)

    rows = {c: 2 * own_count(c) for c in ALL}
    odd = (lax.axis_index("gx") % 2).astype(jnp.int32).reshape(1)
    near, edge, far = in_vmem((X_NEAR[1], 128), (N * len(EDGE), 128), (X_FAR[1], 128))
    outs = in_vmem(*[(TILES[c], 256, 128) for c in ALL]) + (near, near, far)
    scratch = in_vmem((256, 512), (256, 512))
    g1, g2, g3, chip, across, far_own = call(bulk_kernel, (flat,), outs, "own_y", scratch, 12, odd)
    across = swap(across, "gx", 1)
    weights = jnp.asarray(halo_matrix())
    outs = in_vmem((3, 256, 128)) + (near, edge, far)
    d, chip, edge, far = call(
        halo_kernel,
        (above, below, to_down, to_up, weights, chip, far_own),
        outs,
        "halo_y",
        in_vmem((256, 128)),
        4,
        odd,
    )
    edge = swap(edge, "gx", 1)
    chip = swap(chip, "gx", 0)
    far = shift(far, "gx", 2)

    blocks = in_vmem(*[(TILES[c], rows[c] * N, 128) for c in ALL])
    own = call(own_x_kernel, (g1, g2, g3, d), blocks, "own_x", (), 8)
    messages = in_vmem(*[(m[1], 128) for m in (Z_UP, Z_DOWN, Z_UP2, Z_DOWN2)])
    near_x = (chip, across, edge)
    a1, a2, up, down = call(
        functools.partial(x_kernel, (1, 2)), (*own[:2], *near_x), blocks[:2] + messages[:2], "spill_x", (near, near), 6, odd
    )
    a3, up, down, up2, down2 = call(
        functools.partial(x_kernel, (3,)),
        (own[2], *near_x, far, up, down),
        blocks[2:] + messages,
        "spill_x_last",
        (near, near),
        1,
        odd,
    )
    up = shift(up, "gz", 1)
    down = shift(down, "gz", -1)
    up2 = shift(up2, "gz", 2)
    down2 = shift(down2, "gz", -2)

    outs = in_vmem(*[(TILES[c], rows[c], rows[c], 128) for c in ALL])
    own = call(own_z_kernel, (a1, a2, a3), outs, "own_z", (), 8)
    shapes = ((7, 8, 8, 512), (7, 4, 4, 256), (7, 2, 2, 128), (2, 2, 128))
    one, two = pl.pallas_call(
        z_kernel,
        out_shape=tuple(jax.ShapeDtypeStruct(shape, F32) for shape in shapes[:2]),
        in_specs=[VMEM] * 4,
        out_specs=tuple([pl.BlockSpec(memory_space=pltpu.HBM)] * 2),
        scratch_shapes=[*in_vmem(*shapes[:2]), pltpu.SemaphoreType.DMA((5,))],
        compiler_params=PARAMS,
        cost_estimate=pl.CostEstimate(flops=0, transcendentals=0, bytes_accessed=6 * 2**20),
        name="spill_z",
    )(*pinned((*own[:2], up, down)))
    outs = tuple(jax.ShapeDtypeStruct(shape, F32) for shape in shapes[2:])
    three, last = call(z_last_kernel, (own[2], up, down, up2, down2), outs, "spill_z_last", (), 1)
    return one, two, three, last


def solution(mesh):
    return jax.shard_map(
        on_device,
        mesh=mesh,
        in_specs=(P("gz", "gx", "gy"),),
        out_specs=(
            P(None, "gz", "gx", "gy"),
            P(None, "gz", "gx", "gy"),
            P(None, "gz", "gx", "gy"),
            P("gz", "gx", "gy"),
        ),
        check_vma=False,
    )
```
